32 devices in a mesh: rows: 16 (over z, y, core), protos: 2 (over x).
Axes of the slice: x: 2, y: 2, z: 4, core: 2. Of those that a mesh axis runs over, the one named last changes fastest.
Arguments:
- teacher: bfloat16 [1024, 256], P('rows')
- students: bfloat16 [4096, 256], P('rows')
- prototypes: bfloat16 [256, 65536], P(None, 'protos')
- pairing: int32 [4096], P('rows'), may hold values from 0 to 63
- layout: int32 [4096], P('rows'), may hold values from 0 to 15, as said below
Outputs:
- grad_students: float32 [4096, 256], P('rows')
- grad_protos: float32 [256, 65536], P('rows', 'protos')
The draws below stay inside these ranges and needn't reach their ends.
Inputs may be any that keep to these rules, and one draw needn't show every extreme that they name: `layout`: in each aligned block of 256 rows, every value appears exactly 16 times.
All inputs are finite; a program needn't handle non-finite values.
Results may differ from the reference program's by a relative error of at most 0.0003.
The reference program's roundings to bfloat16 on the way (of `w_unit_b`, `tea_unit_b`, `stu_unit_b` and `grad_logits`) count: a program that leaves them out, or rounds other values in their place, can miss the bound.
Values may be sent and summed in bfloat16 or wider, within the bound.
No kernel may reach another device: no remote copies, remote signals or barrier semaphores. Data moves between devices by JAX's collectives and lax.ppermute only.
A program may use at most 192 MiB of HBM per device.

```python
import math
import jax
import jax.numpy as jnp
from jax import lax

D = 256
PROTOS = 65536
TEA_DEV = 64
ITERS = 2
TEACHERS = 1024
STU_DEV = 256
STUDENTS = 4096
BUCKET = 16


cluster_count = 4


def cluster_centers(key):
    raw_centers = jax.random.normal(jax.random.fold_in(key, 101), (cluster_count, D), jnp.float32)
    return raw_centers / jnp.sqrt(jnp.sum(raw_centers * raw_centers, 1, keepdims=True))


def clustered(key, salt, amount):
    cluster_ids = jax.random.randint(jax.random.fold_in(key, salt), (amount,), 0, cluster_count)
    jitter = jax.random.normal(jax.random.fold_in(key, salt + 1), (amount, D), jnp.float32) / math.sqrt(D)
    vectors = 0.85 * cluster_centers(key)[cluster_ids] + 0.5 * jitter
    return vectors


def draw_teacher(key, part):
    return clustered(key, 1, TEACHERS).astype(jnp.bfloat16)


def draw_students(key, part):
    return clustered(key, 11, STUDENTS).astype(jnp.bfloat16)


def draw_prototypes(key, part):
    return clustered(key, 21, PROTOS).T.astype(jnp.bfloat16)


def draw_layout(key, part):
    block_count = STUDENTS // STU_DEV
    groups = STU_DEV // BUCKET
    labels = jnp.repeat(jnp.arange(groups, dtype=jnp.int32), BUCKET)
    block_keys = jax.random.split(jax.random.fold_in(key, 31), block_count)
    mixed = jax.vmap(lambda one_key: jax.random.permutation(one_key, labels))(block_keys)
    return mixed.reshape(-1).astype(jnp.int32)


def place_ends(result, key, smallest, high):
    index_at = [jax.random.randint(jax.random.fold_in(key, axis), (), 0, length) for axis, length in enumerate(result.shape)]
    longest = result.shape.index(max(result.shape))
    beside = index_at[:longest] + [(index_at[longest] + 1) % result.shape[longest]] + index_at[longest + 1:]
    return result.at[tuple(index_at)].set(smallest).at[tuple(beside)].set(high)


def setup_inputs(seed: int = 0) -> dict:
    keys = jax.random.split(jax.random.key(seed), 6)
    teacher = draw_teacher(jax.random.fold_in(keys[5], 71), 0)
    students = draw_students(jax.random.fold_in(keys[5], 71), 0)
    prototypes = draw_prototypes(jax.random.fold_in(keys[5], 71), 0)
    pairing = place_ends(jax.random.randint(keys[3], (STUDENTS,), 0, TEA_DEV), jax.random.fold_in(keys[3], 1), 0, TEA_DEV - 1).astype(jnp.int32)
    layout = draw_layout(jax.random.fold_in(keys[5], 71), 0)
    return {"teacher": teacher, "students": students, "prototypes": prototypes, "pairing": pairing, "layout": layout}


epsilon = 1e-06
teacher_temp = 0.07
student_temp = 0.1
loss_scale = 16.0

def reference(teacher, students, prototypes, pairing, layout):
    weights = prototypes.astype(jnp.float32)
    w_norm = jnp.sqrt(lax.optimization_barrier(jnp.sum(weights * weights, 0)) + epsilon)
    w_unit = weights / w_norm
    w_unit_b = w_unit.astype(jnp.bfloat16)
    tea_full = teacher.astype(jnp.float32)
    tea_unit_b = (tea_full / jnp.sqrt(lax.optimization_barrier(jnp.sum(tea_full * tea_full, 1, keepdims=True)) + epsilon)).astype(jnp.bfloat16)
    tea_block = 256 if TEACHERS % 256 == 0 else TEACHERS
    tea_blocks = tea_unit_b.reshape(TEACHERS // tea_block, tea_block, D)

    def exp_scores(rows_b):
        return jnp.exp(jnp.dot(rows_b, w_unit_b, preferred_element_type=jnp.float32) / teacher_temp)
    row_factor = jnp.ones((TEACHERS,), jnp.float32)
    col_factor = jnp.ones((PROTOS,), jnp.float32)
    for sweep in range(ITERS):

        def add_columns(running, pieces):
            rows_b, factor = pieces
            return (running + lax.optimization_barrier(jnp.sum(exp_scores(rows_b) * factor[:, None], 0)), None)
        colsum, _ = lax.scan(add_columns, jnp.zeros((PROTOS,), jnp.float32), (tea_blocks, row_factor.reshape(-1, tea_block)))
        col_factor = 1.0 / (PROTOS * colsum)
        current = col_factor

        def row_total(rows_b):
            return lax.optimization_barrier(jnp.sum(exp_scores(rows_b) * current[None, :], 1))
        rowsum = lax.map(row_total, tea_blocks).reshape(-1)
        row_factor = 1.0 / (TEACHERS * rowsum)
    row_of = (layout * TEA_DEV + pairing).astype(jnp.int32)
    stu_full = students.astype(jnp.float32)
    u_norm = jnp.sqrt(lax.optimization_barrier(jnp.sum(stu_full * stu_full, 1, keepdims=True)) + epsilon)
    stu_unit = stu_full / u_norm
    stu_unit_b = stu_unit.astype(jnp.bfloat16)
    stu_block = 256 if STUDENTS % 256 == 0 else STUDENTS
    blocks = STUDENTS // stu_block

    def student_step(grad_w_unit, pieces):
        unit_rows, unit_rows_b, norm_rows, row_ids = pieces
        logits = jnp.dot(unit_rows_b, w_unit_b, preferred_element_type=jnp.float32) / student_temp
        exp_logits = jnp.exp(logits)
        denominator = lax.optimization_barrier(jnp.sum(exp_logits, 1, keepdims=True))
        paired = tea_unit_b[row_ids]
        target_rows = TEACHERS * exp_scores(paired) * row_factor[row_ids][:, None] * col_factor[None, :]
        grad_logits = (loss_scale / student_temp * (exp_logits / denominator - target_rows)).astype(jnp.bfloat16)
        grad_unit = jnp.dot(grad_logits, w_unit_b.T, preferred_element_type=jnp.float32)
        grad_rows = (grad_unit - unit_rows * lax.optimization_barrier(jnp.sum(unit_rows * grad_unit, 1, keepdims=True))) / norm_rows
        grad_w_unit = grad_w_unit + jnp.dot(unit_rows_b.T, grad_logits, preferred_element_type=jnp.float32)
        return (grad_w_unit, grad_rows)
    grad_w_unit, grad_blocks = lax.scan(student_step, jnp.zeros((D, PROTOS), jnp.float32), (stu_unit.reshape(blocks, stu_block, D), stu_unit_b.reshape(blocks, stu_block, D), u_norm.reshape(blocks, stu_block, 1), row_of.reshape(blocks, stu_block)))
    grad_students = grad_blocks.reshape(STUDENTS, D)
    grad_protos = (grad_w_unit - w_unit * lax.optimization_barrier(jnp.sum(w_unit * grad_w_unit, 0))) / w_norm
    return (grad_students, grad_protos)
```

```python
import functools

import jax
import jax.numpy as jnp
from jax import lax
from jax.experimental import pallas as pl
from jax.experimental.pallas import tpu as pltpu
from jax.sharding import Mesh, PartitionSpec as P

epsilon = 1e-06
teacher_temp = 0.07
student_temp = 0.1
loss_scale = 16.0

LOG2E = 1.4426950408889634
HALVES = 2
LANES = 128
VMEM = 56 * 1024 * 1024
F32 = jnp.float32
BF16 = jnp.bfloat16
F16 = jnp.float16


def params(*semantics):
    return pltpu.CompilerParams(vmem_limit_bytes=VMEM, dimension_semantics=semantics)


def tile_of(size, want):
    return want if size % want == 0 else size


def unit_rows(rows):
    full = rows.astype(F32)
    return full / jnp.sqrt(jnp.sum(full * full, 1, keepdims=True) + epsilon)


def lane_fold(block):
    total = block[:, :LANES]
    for start in range(LANES, block.shape[1], LANES):
        total = total + block[:, start : start + LANES]
    return total


def row_totals(folded):
    return jnp.sum(jnp.transpose(folded), 0, keepdims=True)


def as_column(row):
    return jnp.transpose(jnp.broadcast_to(row, (LANES, row.shape[1])))[:, :1]


def dot(a, b):
    return jnp.dot(a, b, preferred_element_type=F32)


def denominator_kernel(students_ref, weights_ref, total_ref, unit, folded):
    step = pl.program_id(0)

    @pl.when(step == 0)
    def _():
        unit[...] = unit_rows(students_ref[...]).astype(BF16)
        folded[...] = jnp.zeros_like(folded)

    weights = weights_ref[...].astype(F32)
    inverse = 1.0 / jnp.sqrt(jnp.sum(weights * weights, 0, keepdims=True) + epsilon)
    logits = dot(unit[...], (weights * inverse).astype(BF16))
    folded[...] += lane_fold(jnp.exp2(logits * (LOG2E / student_temp)))

    @pl.when(step == pl.num_programs(0) - 1)
    def _():
        total_ref[...] = row_totals(folded[...])


def local_denominator(students, prototypes):
    rows, width = students.shape
    columns = prototypes.shape[1]
    tile = tile_of(columns, 1024)
    return pl.pallas_call(
        denominator_kernel,
        out_shape=jax.ShapeDtypeStruct((1, rows), F32),
        grid=(columns // tile,),
        in_specs=[
            pl.BlockSpec((rows, width), lambda j: (0, 0)),
            pl.BlockSpec((width, tile), lambda j: (0, j)),
        ],
        out_specs=pl.BlockSpec((1, rows), lambda j: (0, 0)),
        scratch_shapes=[pltpu.VMEM((rows, width), BF16), pltpu.VMEM((rows, LANES), F32)],
        compiler_params=params("arbitrary"),
        cost_estimate=pl.CostEstimate(
            flops=2 * rows * width * columns,
            bytes_accessed=2 * width * columns,
            transcendentals=rows * columns,
        ),
        name="denominator",
    )(students, prototypes)


def sweep_kernel(own_ref, other_ref, weights_ref, *rest, first):
    if first:
        total_ref, factor_ref, unit_ref, folded = rest
    else:
        row_ref, total_ref, factor_ref, folded, column = rest
        unit_ref = None
    half = own_ref.shape[0]
    step = pl.program_id(0)

    @pl.when(step == 0)
    def _():
        if first:
            unit_ref[:half, :] = unit_rows(own_ref[...]).astype(BF16)
            unit_ref[half:, :] = unit_rows(other_ref[...]).astype(BF16)
        else:
            column[...] = jnp.transpose(jnp.broadcast_to(row_ref[...], (LANES, 2 * half)))
        folded[...] = jnp.zeros_like(folded)

    for part in range(2):
        span = slice(part * half, (part + 1) * half)
    units = unit_ref[...] if first else jnp.concatenate([own_ref[...], other_ref[...]], 0)
    scores = jnp.exp2(dot(units, weights_ref[...]) * (LOG2E / teacher_temp))
    weighted = scores if first else scores * column[:, :1]
    factor = 1.0 / jnp.sum(weighted, 0, keepdims=True)
    factor_ref[...] = factor
    folded[...] += lane_fold(scores * factor)

    @pl.when(step == pl.num_programs(0) - 1)
    def _():
        total_ref[...] = row_totals(folded[...])


def sweep(own, other, weights, row_factor=None):
    first = row_factor is None
    half, width = own.shape
    columns = weights.shape[1]
    tile = tile_of(columns, 512)
    whole = lambda j: (0, 0)
    out_shape = [
        jax.ShapeDtypeStruct((1, 2 * half), F32),
        jax.ShapeDtypeStruct((1, columns), F32),
    ]
    out_specs = [
        pl.BlockSpec((1, 2 * half), whole),
        pl.BlockSpec((1, tile), lambda j: (0, j)),
    ]
    in_specs = [
        pl.BlockSpec((half, width), whole),
        pl.BlockSpec((half, width), whole),
        pl.BlockSpec((width, tile), lambda j: (0, j)),
    ]
    scratch = [pltpu.VMEM((2 * half, LANES), F32)]
    operands = [own, other, weights]
    if first:
        out_shape.append(jax.ShapeDtypeStruct((2 * half, width), BF16))
        out_specs.append(pl.BlockSpec((2 * half, width), whole))
    else:
        operands.append(row_factor)
        in_specs.append(pl.BlockSpec((1, 2 * half), whole))
        scratch.append(pltpu.VMEM((2 * half, LANES), F32))
    return pl.pallas_call(
        functools.partial(sweep_kernel, first=first),
        out_shape=out_shape,
        grid=(columns // tile,),
        in_specs=in_specs,
        out_specs=out_specs,
        scratch_shapes=scratch,
        compiler_params=params("arbitrary"),
        cost_estimate=pl.CostEstimate(
            flops=4 * half * width * columns,
            bytes_accessed=2 * width * (columns + 2 * half),
            transcendentals=2 * half * columns,
        ),
        name="sweep",
    )(*operands)


def pair_kernel(half_ref, own_ref, other_ref, index_ref, teacher_ref, unit_ref, turned_ref, paired_ref):
    rows = own_ref.shape[1]
    teachers = teacher_ref.shape[0]
    places = lax.broadcasted_iota(jnp.int32, (rows, teachers), 1).astype(F32)
    for part, ref in enumerate((own_ref, other_ref)):
        unit = unit_rows(ref[0])
        unit_ref[0, part] = unit.astype(BF16)
        turned_ref[0, part] = jnp.transpose(unit).astype(BF16)
        chosen = as_column(index_ref[0, part]) == places
        paired_ref[0, part] = dot(
            jnp.where(chosen, 1.0, 0.0).astype(BF16), teacher_ref[...]
        ).astype(BF16)


def pair(half, own, other, index, teachers):
    groups, count, width = own.shape
    tile = tile_of(count, 256)
    held = lambda g, b, half_ref: (lax.rem(g + half_ref[0] + 1, groups), b, 0)
    rows = lambda g, b, half_ref: (g, 0, b, 0)
    lanes = lambda g, b, half_ref: (g, 0, 0, b)
    return pl.pallas_call(
        pair_kernel,
        out_shape=[
            jax.ShapeDtypeStruct((groups, 2, count, width), BF16),
            jax.ShapeDtypeStruct((groups, 2, width, count), BF16),
            jax.ShapeDtypeStruct((groups, 2, count, width), BF16),
        ],
        grid_spec=pltpu.PrefetchScalarGridSpec(
            num_scalar_prefetch=1,
            grid=(groups, count // tile),
            in_specs=[
                pl.BlockSpec((1, tile, width), held),
                pl.BlockSpec((1, tile, width), held),
                pl.BlockSpec((1, 2, 1, tile), lanes),
                pl.BlockSpec(teachers.shape, lambda g, b, half_ref: (0, 0)),
            ],
            out_specs=[
                pl.BlockSpec((1, 2, tile, width), rows),
                pl.BlockSpec((1, 2, width, tile), lanes),
                pl.BlockSpec((1, 2, tile, width), rows),
            ],
        ),
        compiler_params=params("arbitrary", "arbitrary"),
        cost_estimate=pl.CostEstimate(
            flops=4 * groups * count * width * teachers.shape[0],
            bytes_accessed=16 * groups * count * width,
            transcendentals=0,
        ),
        name="pair",
    )(half, own, other, index.reshape(groups, 2, 1, count), teachers)


def gradient_kernel(
    unit_ref,
    turned_ref,
    paired_ref,
    total_ref,
    index_ref,
    row_ref,
    column_ref,
    weights_ref,
    flipped_ref,
    raw_ref,
    norm_ref,
    student_ref,
    proto_ref,
    scale,
    *,
    tile,
    skipped,
):
    block, step = pl.program_id(0), pl.program_id(1)
    rows = unit_ref.shape[2]
    teachers = row_ref.shape[1]
    span = pl.ds(pl.multiple_of(step * tile, tile), tile)

    @pl.when(step == 0)
    def _():
        ones = jnp.ones((rows, LANES), F32)
        scale[0] = as_column(loss_scale / student_temp / total_ref[...]) * ones
        places = lax.broadcasted_iota(jnp.int32, (rows, teachers), 1).astype(F32)
        chosen = jnp.where(as_column(index_ref[...]) == places, row_ref[...], 0.0)
        scale[1] = jnp.sum(chosen, 1, keepdims=True) * (loss_scale / student_temp) * ones

    weights = weights_ref[:, span]
    student = jnp.exp2(dot(unit_ref[0, 0], weights) * (LOG2E / student_temp)) * scale[0][:, :1]
    target = jnp.exp2(dot(paired_ref[0, 0], weights) * (LOG2E / teacher_temp)) * scale[1][:, :1]
    grad = (student - target * column_ref[:, span]).astype(BF16)

    @pl.when(block >= skipped)
    def _():
        share = dot(grad, flipped_ref[span, :])

        @pl.when(step == 0)
        def _():
            student_ref[...] = share

        @pl.when(step > 0)
        def _():
            student_ref[...] += share

    share = dot(turned_ref[0, 0], grad)

    @pl.when(block == 0)
    def _():
        proto_ref[:, span] = share

    @pl.when(block > 0)
    def _():
        proto_ref[:, span] += share

    @pl.when(block == pl.num_programs(0) - 1)
    def _():
        norm = norm_ref[:, span]
        unit = raw_ref[:, span].astype(F32) / norm
        grads = proto_ref[:, span]
        proto_ref[:, span] = (grads - unit * jnp.sum(unit * grads, 0, keepdims=True)) / norm


def gradients(unit, turned, paired, total, index, row_factor, col_factor, weights, raw, norm):
    groups, _, count, width = unit.shape
    columns = weights.shape[1]
    size = tile_of(count, 512)
    tile = tile_of(columns, 512)
    each = count // size
    blocks = groups * 2 * each
    skipped = (groups - 1) * 2 * each
    place = lambda p, j: (p // (2 * each), (p // each) % 2, p % each, 0)
    across = lambda p, j: (p // (2 * each), (p // each) % 2, 0, p % each)
    whole = lambda p, j: (0, 0)
    return pl.pallas_call(
        functools.partial(gradient_kernel, tile=tile, skipped=skipped),
        out_shape=[
            jax.ShapeDtypeStruct((2 * count, width), F32),
            jax.ShapeDtypeStruct((width, columns), F32),
        ],
        grid=(blocks, columns // tile),
        in_specs=[
            pl.BlockSpec((1, 1, size, width), place),
            pl.BlockSpec((1, 1, width, size), across),
            pl.BlockSpec((1, 1, size, width), place),
            pl.BlockSpec((1, size), lambda p, j: (0, p)),
            pl.BlockSpec((1, size), lambda p, j: (0, p)),
            pl.BlockSpec(row_factor.shape, whole),
            pl.BlockSpec((1, columns), whole),
            pl.BlockSpec((width, columns), whole),
            pl.BlockSpec((columns, width), whole),
            pl.BlockSpec((width, columns), whole),
            pl.BlockSpec((1, columns), whole),
        ],
        out_specs=[
            pl.BlockSpec((size, width), lambda p, j: (jnp.maximum(p - skipped, 0), 0)),
            pl.BlockSpec((width, columns), whole),
        ],
        scratch_shapes=[pltpu.VMEM((2, size, LANES), F32)],
        compiler_params=params("arbitrary", "arbitrary"),
        cost_estimate=pl.CostEstimate(
            flops=8 * groups * 2 * count * width * columns,
            bytes_accessed=8 * width * columns,
            transcendentals=4 * groups * count * columns,
        ),
        name="gradients",
    )(
        unit,
        turned,
        paired,
        total.reshape(1, -1),
        index.reshape(1, -1),
        row_factor,
        col_factor,
        weights,
        jnp.transpose(weights),
        raw,
        norm,
    )


def swap(value, axis):
    return lax.ppermute(value, axis, [(0, 1), (1, 0)])


def exchange(value, axes):
    return lax.all_to_all(value, axes, split_axis=0, concat_axis=0, tiled=True)


def gather(value, axes, count):
    return exchange(jnp.tile(value, (count,) + (1,) * (value.ndim - 1)), axes)


def body(teacher, students, prototypes, pairing, layout):
    halves, chips, protos = lax.axis_size("half"), lax.axis_size("chip"), lax.axis_size("protos")
    half, chip, core, proto = (lax.axis_index(a) for a in ("half", "chip", "core", "protos"))
    everyone = ("half", "chip", "core", "protos")
    devices = halves * chips * 2 * protos
    all_chips = halves * chips
    width, held = prototypes.shape
    tea_count, stu_count = teacher.shape[0], students.shape[0]
    teachers = tea_count * all_chips * 2
    columns = held // (chips * 2)
    sweep_columns = columns // halves

    def mine_first(pair_of):
        return jnp.where(core == 0, pair_of, pair_of[::-1])

    tea_own = gather(teacher, ("half", "chip"), all_chips)
    tea_other = swap(tea_own, "core")
    stu_own = gather(students, ("half", "chip"), all_chips)
    stu_other = swap(stu_own, "core")

    raw = lax.dynamic_slice_in_dim(prototypes, (chip * 2 + core) * columns, columns, 1)
    full = raw.astype(F32)
    w_norm = jnp.sqrt(jnp.sum(full * full, 0, keepdims=True) + epsilon)
    weights = (full / w_norm).astype(BF16)
    sweep_weights = lax.dynamic_slice_in_dim(weights, half * sweep_columns, sweep_columns, 1)

    own_total = local_denominator(students, prototypes)
    own_index = (layout % 2) * (all_chips * tea_count) + (layout // 2) * tea_count + pairing

    row_part, _, tea_unit = sweep(tea_own, tea_other, sweep_weights)
    parcel = jnp.concatenate(
        [
            mine_first(row_part.reshape(2, -1)).reshape(-1),
            own_total.reshape(-1),
            own_index.astype(F32),
        ]
    )
    length = parcel.shape[0]
    parcel = jnp.broadcast_to(parcel.reshape(1, length // LANES, LANES), (devices, length // LANES, LANES))
    parcels = exchange(parcel, everyone).reshape(devices, length)
    row_factor = 1.0 / jnp.sum(parcels[:, :teachers], 0)
    row_factor = mine_first(row_factor.reshape(2, -1)).reshape(1, teachers)

    def in_order(values):
        values = jnp.transpose(values, (2, 0, 1, 3))
        values = mine_first(values)
        if halves > 1:
            values = jnp.roll(values, -(half + 1), 1)
        return jnp.transpose(values, (1, 0, 2, 3)).reshape(halves, 2, chips * stu_count)

    by_sender = parcels[:, teachers:].reshape(halves, chips, 2, protos, 2, stu_count)
    total = in_order(jnp.sum(by_sender[:, :, :, :, 0], 3))
    index = in_order(by_sender[:, :, :, 0, 1])
    index = jnp.where(core == 0, index, (index + teachers // 2) % teachers)

    tea_half = teachers // 2
    row_part, col_factor = sweep(tea_unit[:tea_half], tea_unit[tea_half:], sweep_weights, row_factor)
    parcel = mine_first(row_part.reshape(2, -1)).reshape(1, teachers // LANES, LANES)
    parcels = exchange(jnp.broadcast_to(parcel, (devices,) + parcel.shape[1:]), everyone)
    row_factor = 1.0 / jnp.sum(parcels.reshape(devices, teachers), 0)
    row_factor = mine_first(row_factor.reshape(2, -1)).reshape(1, teachers)
    if halves == 2:
        far = swap(col_factor, "half")
        col_factor = jnp.concatenate(
            [jnp.where(half == 0, col_factor, far), jnp.where(half == 0, far, col_factor)], 1
        )

    unit, turned, paired = pair(
        half.reshape(1),
        stu_own.reshape(halves, -1, width),
        stu_other.reshape(halves, -1, width),
        index,
        tea_unit,
    )
    student_part, proto_part = gradients(
        unit, turned, paired, total, index, row_factor, col_factor, weights, raw, w_norm
    )

    share = width // (all_chips * 2)
    kept = lax.dynamic_slice_in_dim(proto_part, half * (width // halves), width // halves, 0)
    power = jnp.floor(jnp.log2(jnp.maximum(jnp.max(jnp.abs(kept)), 1e-30))) - 13.0
    sent = (kept * jnp.exp2(-power)).astype(F16).reshape(chips * 2, share, columns)
    sent = jnp.concatenate(
        [sent, jnp.broadcast_to(power.astype(F16), (chips * 2, share, LANES))], 2
    )
    came = exchange(sent, ("chip", "core"))
    powers = jnp.exp2(came[:, :, columns : columns + 1].astype(F32))
    grad_protos = jnp.transpose(came[:, :, :columns].astype(F32) * powers, (1, 0, 2))
    grad_protos = grad_protos.reshape(share, held)

    student_part = student_part.reshape(2, chips * stu_count, width)
    summed = student_part[0] + swap(student_part[1], "core")
    near = lax.dynamic_slice_in_dim(stu_own, half * chips * stu_count, chips * stu_count, 0)
    near = unit_rows(near)
    summed = summed - near * jnp.sum(near * summed, 1, keepdims=True)
    sent = (summed * 128.0).astype(F16).reshape(chips * protos, stu_count // protos, width)
    came = exchange(sent, ("chip", "protos"))
    part = jnp.sum(came.astype(F32), 0) * (1.0 / 128.0)
    if protos == 2:
        far = swap(part, "protos")
        grad_unit = jnp.concatenate(
            [jnp.where(proto == 0, part, far), jnp.where(proto == 0, far, part)], 0
        )
    else:
        grad_unit = gather(part, "protos", protos)
    stu_full = students.astype(F32)
    u_norm = jnp.sqrt(jnp.sum(stu_full * stu_full, 1, keepdims=True) + epsilon)
    return (grad_unit / u_norm, grad_protos)


def solution(mesh):
    rows, protos = mesh.shape["rows"], mesh.shape["protos"]
    halves = HALVES
    split = Mesh(
        mesh.devices.reshape(halves, rows // (2 * halves), 2, protos),
        ("half", "chip", "core", "protos"),
    )
    over_rows = ("half", "chip", "core")
    in_specs = (
        P(over_rows, None),
        P(over_rows, None),
        P(None, "protos"),
        P(over_rows),
        P(over_rows),
    )
    out_specs = (P(over_rows, None), P(over_rows, "protos"))
    return jax.shard_map(
        body, mesh=split, in_specs=in_specs, out_specs=out_specs, check_vma=False
    )
```

```python
import functools

import jax
import jax.numpy as jnp
from jax import lax
from jax.experimental import pallas as pl
from jax.experimental.pallas import tpu as pltpu
from jax.sharding import Mesh, PartitionSpec as P

epsilon = 1e-06
teacher_temp = 0.07
student_temp = 0.1
loss_scale = 16.0

LOG2E = 1.4426950408889634
HALVES = 2
LANES = 128
MIB = 1024 * 1024
F32 = jnp.float32
BF16 = jnp.bfloat16
F16 = jnp.float16


def params(limit):
    return pltpu.CompilerParams(
        vmem_limit_bytes=limit * MIB, dimension_semantics=("arbitrary",)
    )


def tile_of(size, want):
    return want if size % want == 0 else size


def unit_rows(rows):
    full = rows.astype(F32)
    return full * (1.0 / jnp.sqrt(jnp.sum(full * full, 1, keepdims=True) + epsilon))


def lane_fold(block):
    total = block[:, :LANES]
    for start in range(LANES, block.shape[1], LANES):
        total = total + block[:, start : start + LANES]
    return total


def widen(column, width):
    return jnp.concatenate([column] * (width // LANES), 1)


def as_columns(values):
    return jnp.concatenate(
        [
            jnp.transpose(jnp.broadcast_to(values[i : i + 1], (LANES, LANES)))
            for i in range(values.shape[0])
        ],
        0,
    )


def as_rows(folded):
    return jnp.concatenate(
        [
            jnp.sum(jnp.transpose(folded[i : i + LANES]), 0, keepdims=True)
            for i in range(0, folded.shape[0], LANES)
        ],
        0,
    )


def dot(a, b):
    return jnp.dot(a, b, preferred_element_type=F32)


def reverse_bits(place, count):
    bits = count.bit_length() - 1
    return sum(((place >> i) & 1) << (bits - 1 - i) for i in range(bits))


class Layout:
    def __init__(self, halves, chips, protos, tea_count, stu_count):
        self.halves, self.chips, self.protos = halves, chips, protos
        self.devices = halves * chips * 2 * protos
        self.tea_rows = halves * chips * tea_count
        self.tea_lanes = 2 * self.tea_rows // LANES
        self.stu_lanes = stu_count // LANES
        self.stu_count = stu_count
        self.block = chips * stu_count

    def sender(self, where, other_half, other_core, place):
        half, chip, core = where[0], where[1], where[2]
        source = (half ^ other_half) * self.chips + (chip ^ reverse_bits(place, self.chips))
        return (source * 2 + (core ^ other_core)) * self.protos

    def teacher_totals(self, where, parcels_ref):
        sums = [None, None]
        for number in range(self.devices):
            side = (number // self.protos) % 2
            piece = parcels_ref[number, : self.tea_lanes]
            sums[side] = piece if sums[side] is None else sums[side] + piece
        cut = self.tea_lanes // 2
        turned = [jnp.concatenate([s[cut:], s[:cut]], 0) for s in sums]
        return jnp.where(where[2] == 0, sums[0] + turned[1], sums[1] + turned[0])


def columns_kernel(where_ref, raw_ref, unit_ref, flipped_ref, norm_ref, copy_ref):
    copy_ref[...] = raw_ref[...]
    full = raw_ref[...].astype(F32)
    norm = jnp.sqrt(jnp.sum(full * full, 0, keepdims=True) + epsilon)
    unit = full * (1.0 / norm)
    unit_ref[...] = unit.astype(BF16)
    flipped_ref[...] = jnp.transpose(unit.astype(BF16))
    norm_ref[...] = norm


def unit_columns(where, prototypes, columns):
    width = prototypes.shape[0]
    tile = tile_of(columns, 1024)
    steps = columns // tile
    return pl.pallas_call(
        columns_kernel,
        out_shape=[
            jax.ShapeDtypeStruct((width, columns), BF16),
            jax.ShapeDtypeStruct((columns, width), BF16),
            jax.ShapeDtypeStruct((1, columns), F32),
            jax.ShapeDtypeStruct((width, columns), BF16),
        ],
        grid_spec=pltpu.PrefetchScalarGridSpec(
            num_scalar_prefetch=1,
            grid=(steps,),
            in_specs=[
                pl.BlockSpec((width, tile), lambda j, w: (0, (w[1] * 2 + w[2]) * steps + j))
            ],
            out_specs=[
                pl.BlockSpec((width, tile), lambda j, w: (0, j)),
                pl.BlockSpec((tile, width), lambda j, w: (j, 0)),
                pl.BlockSpec((1, tile), lambda j, w: (0, j)),
                pl.BlockSpec((width, tile), lambda j, w: (0, j)),
            ],
        ),
        compiler_params=params(50),
        cost_estimate=pl.CostEstimate(
            flops=8 * width * columns, bytes_accessed=6 * width * columns, transcendentals=0
        ),
        name="unit_columns",
    )(where, prototypes)


def denominator_kernel(students_ref, weights_ref, total_ref, unit, folded, *, sub):
    step = pl.program_id(0)

    @pl.when(step == 0)
    def _():
        unit[...] = unit_rows(students_ref[...]).astype(BF16)
        folded[...] = jnp.zeros_like(folded)

    def scaled(start):
        weights = weights_ref[:, start : start + sub].astype(F32)
        inverse = 1.0 / jnp.sqrt(jnp.sum(weights * weights, 0, keepdims=True) + epsilon)
        return (weights * inverse).astype(BF16)

    total = folded[...]
    for start in range(0, weights_ref.shape[1], sub):
        logits = dot(unit[...], scaled(start))
        total = total + lane_fold(jnp.exp2(logits * (LOG2E / student_temp)))
    folded[...] = total

    @pl.when(step == pl.num_programs(0) - 1)
    def _():
        total_ref[...] = as_rows(folded[...])


def local_denominator(students, prototypes, part, parts):
    rows, width = students.shape
    columns = prototypes.shape[1] // parts
    tile = tile_of(columns, 4096)
    steps = columns // tile
    return pl.pallas_call(
        functools.partial(denominator_kernel, sub=tile_of(tile, 512)),
        out_shape=jax.ShapeDtypeStruct((rows // LANES, LANES), F32),
        grid=(steps,),
        in_specs=[
            pl.BlockSpec((rows, width), lambda j: (0, 0)),
            pl.BlockSpec((width, tile), lambda j: (0, part * steps + j)),
        ],
        out_specs=pl.BlockSpec((rows // LANES, LANES), lambda j: (0, 0)),
        scratch_shapes=[pltpu.VMEM((rows, width), BF16), pltpu.VMEM((rows, LANES), F32)],
        compiler_params=params(50),
        cost_estimate=pl.CostEstimate(
            flops=2 * rows * width * columns,
            bytes_accessed=2 * width * columns,
            transcendentals=rows * columns,
        ),
        name="denominator",
    )(students, prototypes)


def sweep_totals(units, weights_ref, column, sub, factor_ref):
    folded = jnp.zeros((units.shape[0], LANES), F32)
    for start in range(0, weights_ref.shape[1], sub):
        scores = jnp.exp2(dot(units, weights_ref[:, start : start + sub]) * (LOG2E / teacher_temp))
        weighted = scores if column is None else scores * widen(column, sub)
        factor = 1.0 / jnp.sum(weighted, 0, keepdims=True)
        if factor_ref is not None:
            factor_ref[:, start : start + sub] = factor
        folded = folded + lane_fold(scores * factor)
    return as_rows(folded)


def first_sweep_kernel(
    where_ref, own_ref, other_ref, weights_ref, pairing_ref, layout_ref, parcel_ref, unit_ref, *, plan, sub
):
    half = own_ref.shape[0]
    unit_ref[:half, :] = unit_rows(own_ref[...]).astype(BF16)
    unit_ref[half:, :] = unit_rows(other_ref[...]).astype(BF16)
    totals = sweep_totals(unit_ref[...], weights_ref, None, sub, None)
    parcel_ref[:, : plan.tea_lanes, :] = jnp.broadcast_to(
        totals[None], (plan.devices,) + totals.shape
    )
    each = plan.tea_rows // (plan.halves * plan.chips)
    layout = layout_ref[...]
    index = (layout & 1) * half + (layout >> 1) * each + pairing_ref[...]
    index = index.astype(F32)
    for i in range(plan.stu_lanes):
        parcel_ref[:, plan.tea_lanes + i, :] = jnp.broadcast_to(
            index[:, i * LANES : (i + 1) * LANES], (plan.devices, LANES)
        )


def second_sweep_kernel(
    where_ref, unit_ref, weights_ref, came_ref, near_ref, far_ref, parcel_ref, factor_ref, *, plan, sub
):
    where = (where_ref[0], where_ref[1], where_ref[2])
    column = as_columns(1.0 / plan.teacher_totals(where, came_ref))
    totals = sweep_totals(unit_ref[...], weights_ref, column, sub, factor_ref)
    totals = jnp.concatenate([totals, near_ref[...] + far_ref[...]], 0)
    parcel_ref[...] = jnp.broadcast_to(totals[None], (plan.devices,) + totals.shape)


def sweep_call(kernel, plan, where, operands, weights_at, columns, out_shape, name):
    width = operands[0].shape[1]

    def spec(number, array):
        if number == weights_at:
            return pl.BlockSpec((width, columns), lambda i, w: (0, w[0]))
        return pl.BlockSpec(array.shape, lambda i, w: (0,) * len(array.shape))

    return pl.pallas_call(
        functools.partial(kernel, plan=plan, sub=tile_of(columns, 256)),
        out_shape=out_shape,
        grid_spec=pltpu.PrefetchScalarGridSpec(
            num_scalar_prefetch=1,
            grid=(1,),
            in_specs=[spec(i, a) for i, a in enumerate(operands)],
            out_specs=[
                pl.BlockSpec(o.shape, functools.partial(lambda n, i, w: (0,) * n, len(o.shape)))
                for o in out_shape
            ],
        ),
        compiler_params=params(16),
        cost_estimate=pl.CostEstimate(
            flops=4 * plan.tea_rows * width * columns,
            bytes_accessed=2 * width * (columns + 2 * plan.tea_rows),
            transcendentals=2 * plan.tea_rows * columns,
        ),
        name=name,
    )(where, *operands)


def pair_kernel(where_ref, own_ref, other_ref, came_ref, teacher_ref, unit_ref, turned_ref, paired_ref, *, plan):
    where = (where_ref[0], where_ref[1], where_ref[2])
    apart = plan.halves - 1 - pl.program_id(0)
    teachers = teacher_ref.shape[0]
    count = plan.stu_count
    lane = lax.broadcasted_iota(jnp.int32, (count, LANES), 1).astype(F32)
    for side, ref in enumerate((own_ref, other_ref)):
        for place in range(plan.chips):
            rows = slice(place * count, (place + 1) * count)
            unit = unit_rows(ref[place, 0]).astype(BF16)
            unit_ref[0, side, rows, :] = unit
            turned_ref[0, side, :, rows] = jnp.transpose(unit)
            sender = plan.sender(where, apart, side, place)
            index = as_columns(came_ref[sender, plan.tea_lanes :, :])
            index = index + jnp.where(where[2] == 0, 0.0, float(teachers // 2))
            index = jnp.where(index >= teachers, index - teachers, index)
            chosen = jnp.concatenate(
                [
                    jnp.where(index == lane + start, 1.0, 0.0).astype(BF16)
                    for start in range(0, teachers, LANES)
                ],
                1,
            )
            paired_ref[0, side, rows, :] = dot(chosen, teacher_ref[...]).astype(BF16)


def pair(plan, where, own, other, came, teachers):
    width = own.shape[3]
    held = pl.BlockSpec(
        (plan.chips, 1, plan.stu_count, width), lambda g, w: (0, plan.halves - 1 - g, 0, 0)
    )
    rows = pl.BlockSpec((1, 2, plan.block, width), lambda g, w: (g, 0, 0, 0))
    return pl.pallas_call(
        functools.partial(pair_kernel, plan=plan),
        out_shape=[
            jax.ShapeDtypeStruct((plan.halves, 2, plan.block, width), BF16),
            jax.ShapeDtypeStruct((plan.halves, 2, width, plan.block), BF16),
            jax.ShapeDtypeStruct((plan.halves, 2, plan.block, width), BF16),
        ],
        grid_spec=pltpu.PrefetchScalarGridSpec(
            num_scalar_prefetch=1,
            grid=(plan.halves,),
            in_specs=[
                held,
                held,
                pl.BlockSpec(came.shape, lambda g, w: (0, 0, 0)),
                pl.BlockSpec(teachers.shape, lambda g, w: (0, 0)),
            ],
            out_specs=[
                rows,
                pl.BlockSpec((1, 2, width, plan.block), lambda g, w: (g, 0, 0, 0)),
                rows,
            ],
        ),
        compiler_params=params(56),
        cost_estimate=pl.CostEstimate(
            flops=4 * plan.halves * plan.block * width * teachers.shape[0],
            bytes_accessed=16 * plan.halves * plan.block * width,
            transcendentals=0,
        ),
        name="pair",
    )(where, own, other, came, teachers)


def fill_scale(plan, where, apart, side, first_ref, second_ref, row_factor, scale):
    teachers = plan.tea_lanes * LANES
    places = lax.broadcasted_iota(jnp.int32, (teachers, LANES), 0).astype(F32)
    own_first = jnp.where(where[2] == 0, 0.0, float(teachers // 2))
    for place in range(plan.chips):
        rows = slice(place * plan.stu_count, (place + 1) * plan.stu_count)
        sender = plan.sender(where, apart, side, place)
        total = second_ref[sender, plan.tea_lanes :, :]
        for proto in range(1, plan.protos):
            total = total + second_ref[sender + proto, plan.tea_lanes :, :]
        scale[0, rows, :] = as_columns((loss_scale / student_temp) / total)
        index = first_ref[sender, plan.tea_lanes :, :] + own_first
        index = jnp.where(index >= teachers, index - teachers, index)
        found = [
            jnp.sum(jnp.where(index[i : i + 1] == places, row_factor[...], 0.0), 0, keepdims=True)
            for i in range(plan.stu_lanes)
        ]
        scale[1, rows, :] = as_columns(jnp.concatenate(found, 0))


def gradient_products(
    unit_ref, turned_ref, paired_ref, factor_ref, weights_ref, flipped_ref, shares_ref, scale,
    grads, sub, fresh,
):
    columns = weights_ref.shape[1]
    tile = tile_of(columns, 4 * sub)

    def products(step, shares):
        base = pl.multiple_of(step * tile, tile)

        def logits(start):
            weights = weights_ref[:, pl.ds(base + start, sub)]
            return dot(unit_ref[0, 0], weights), dot(paired_ref[0, 0], weights)

        ahead = logits(0)
        for start in range(0, tile, sub):
            student, target = ahead
            if start + sub < tile:
                ahead = logits(start + sub)
            span = pl.ds(base + start, sub)
            student = jnp.exp2(student * (LOG2E / student_temp)) * widen(scale[0], sub)
            target = jnp.exp2(target * (LOG2E / teacher_temp)) * (
                widen(scale[1], sub) * factor_ref[:, span]
            )
            grad = (student - target).astype(BF16)
            if shares_ref is not None:
                share = dot(grad, flipped_ref[span, :])
                shares = share if shares is None else shares + share
            share = dot(turned_ref[0, 0], grad)
            grads[:, span] = jnp.where(fresh, 0.0, grads[:, span]) + share
        return shares

    @pl.loop(0, columns // tile)
    def _(step):
        shares = products(step, None)
        if shares_ref is not None:
            shares_ref[...] = jnp.where(step == 0, 0.0, shares_ref[...]) + shares


def near_kernel(
    where_ref,
    unit_ref,
    turned_ref,
    paired_ref,
    first_ref,
    second_ref,
    factor_ref,
    weights_ref,
    flipped_ref,
    own_raw_ref,
    other_raw_ref,
    own_ref,
    other_ref,
    grads_ref,
    scale,
    shares,
    row_factor,
    *,
    plan,
    sub,
):
    where = (where_ref[0], where_ref[1], where_ref[2])
    side = pl.program_id(0)
    count = plan.stu_count

    @pl.when(side == 0)
    def _():
        row_factor[...] = as_columns(
            (loss_scale / student_temp) / plan.teacher_totals(where, second_ref)
        )

    fill_scale(plan, where, 0, side, first_ref, second_ref, row_factor, scale)
    gradient_products(
        unit_ref, turned_ref, paired_ref, factor_ref, weights_ref, flipped_ref, shares, scale,
        grads_ref, sub, side == 0,
    )

    def finish(raw_ref, out_ref):
        for place in range(plan.chips):
            rows = slice(place * count, (place + 1) * count)
            chip = where[1] ^ reverse_bits(place, plan.chips)
            unit = unit_rows(raw_ref[place, 0])
            share = shares[rows]
            share = share - unit * jnp.sum(unit * share, 1, keepdims=True)
            out_ref[pl.ds(pl.multiple_of(chip * count, count), count), :] = share

    @pl.when(side == 0)
    def _():
        finish(own_raw_ref, own_ref)

    @pl.when(side == 1)
    def _():
        finish(other_raw_ref, other_ref)


def whole_spec(array):
    return pl.BlockSpec(
        array.shape, lambda p, w: (0,) * array.ndim, pipeline_mode=pl.Buffered(1)
    )


def near_gradients(plan, where, unit, turned, paired, first, second, factor, weights, flipped, own, other):
    width, columns = weights.shape
    last = plan.halves - 1
    rows = pl.BlockSpec((1, 1, plan.block, width), lambda p, w: (last, p, 0, 0))
    raw = pl.BlockSpec(
        (plan.chips, 1, plan.stu_count, width),
        lambda p, w: (0, 0, 0, 0),
        pipeline_mode=pl.Buffered(1),
    )
    students = jax.ShapeDtypeStruct((plan.block, width), F32)
    out_shape = [students, students, jax.ShapeDtypeStruct((width, columns), F32)]
    return pl.pallas_call(
        functools.partial(near_kernel, plan=plan, sub=tile_of(columns, 256)),
        out_shape=out_shape,
        grid_spec=pltpu.PrefetchScalarGridSpec(
            num_scalar_prefetch=1,
            grid=(2,),
            in_specs=[
                rows,
                pl.BlockSpec((1, 1, width, plan.block), lambda p, w: (last, p, 0, 0)),
                rows,
                whole_spec(first),
                whole_spec(second),
                whole_spec(factor),
                whole_spec(weights),
                whole_spec(flipped),
                raw,
                raw,
            ],
            out_specs=[whole_spec(o) for o in out_shape],
            scratch_shapes=[
                pltpu.VMEM((2, plan.block, LANES), F32),
                pltpu.VMEM((plan.block, width), F32),
                pltpu.VMEM((plan.tea_lanes * LANES, LANES), F32),
            ],
        ),
        compiler_params=params(56),
        cost_estimate=pl.CostEstimate(
            flops=16 * plan.block * width * columns,
            bytes_accessed=8 * width * columns,
            transcendentals=4 * plan.block * columns,
        ),
        name="near_gradients",
    )(where, unit, turned, paired, first, second, factor, weights, flipped, own, other)


def far_kernel(
    where_ref,
    unit_ref,
    turned_ref,
    paired_ref,
    first_ref,
    second_ref,
    factor_ref,
    weights_ref,
    raw_ref,
    norm_ref,
    before_ref,
    proto_ref,
    scale,
    grads,
    row_factor,
    *,
    plan,
    sub,
):
    where = (where_ref[0], where_ref[1], where_ref[2])
    block = pl.program_id(0)
    columns = weights_ref.shape[1]

    @pl.when(block == 0)
    def _():
        row_factor[...] = as_columns(
            (loss_scale / student_temp) / plan.teacher_totals(where, second_ref)
        )
        grads[...] = before_ref[...]

    fill_scale(
        plan, where, plan.halves - 1 - block // 2, block % 2, first_ref, second_ref, row_factor, scale
    )
    gradient_products(
        unit_ref, turned_ref, paired_ref, factor_ref, weights_ref, None, None, scale, grads, sub,
        False,
    )

    @pl.when(block == pl.num_programs(0) - 1)
    def _():
        kept = grads.shape[0] // plan.halves
        mine = pl.ds(pl.multiple_of(where[0] * kept, kept), kept)
        largest = jnp.zeros((kept, LANES), F32)
        for start in range(0, columns, sub):
            span = slice(start, start + sub)
            inverse = 1.0 / norm_ref[:, span]
            unit = raw_ref[:, span].astype(F32) * inverse
            along = jnp.sum(unit * grads[:, span], 0, keepdims=True)
            unit = raw_ref[mine, span].astype(F32) * inverse
            ready = (grads[mine, span] - unit * along) * inverse
            proto_ref[:, span] = ready
            ready = jnp.abs(ready)
            for i in range(0, sub, LANES):
                largest = jnp.maximum(largest, ready[:, i : i + LANES])
        largest = jnp.maximum(jnp.max(jnp.max(largest, 0, keepdims=True), 1, keepdims=True), 1e-30)
        power = jnp.floor(jnp.log2(largest)) - 13.0
        shrink = jnp.exp2(-power)
        for start in range(0, columns, sub):
            span = slice(start, start + sub)
            proto_ref[:, span] = proto_ref[:, span] * shrink
        proto_ref[:, columns:] = jnp.broadcast_to(power, (kept, LANES))


def far_gradients(
    plan, where, part, unit, turned, paired, first, second, factor, weights, raw, norm, before
):
    width = weights.shape[0]
    parts = plan.halves
    columns = weights.shape[1] // parts
    rows = pl.BlockSpec((1, 1, plan.block, width), lambda p, w: (p // 2, p % 2, 0, 0))
    span = lambda p, w: (0, part)
    kept = width // plan.halves
    return pl.pallas_call(
        functools.partial(far_kernel, plan=plan, sub=tile_of(columns, 256)),
        out_shape=jax.ShapeDtypeStruct((kept, columns + LANES), F32),
        grid_spec=pltpu.PrefetchScalarGridSpec(
            num_scalar_prefetch=1,
            grid=(2 * (plan.halves - 1),),
            in_specs=[
                rows,
                pl.BlockSpec((1, 1, width, plan.block), lambda p, w: (p // 2, p % 2, 0, 0)),
                rows,
                whole_spec(first),
                whole_spec(second),
                pl.BlockSpec((1, columns), span),
                pl.BlockSpec((width, columns), span),
                pl.BlockSpec((width, columns), span),
                pl.BlockSpec((1, columns), span),
                pl.BlockSpec((width, columns), span),
            ],
            out_specs=pl.BlockSpec((kept, columns + LANES), lambda p, w: (0, 0)),
            scratch_shapes=[
                pltpu.VMEM((2, plan.block, LANES), F32),
                pltpu.VMEM((width, columns), F32),
                pltpu.VMEM((plan.tea_lanes * LANES, LANES), F32),
            ],
        ),
        compiler_params=params(56),
        cost_estimate=pl.CostEstimate(
            flops=12 * (plan.halves - 1) * plan.block * width * columns,
            bytes_accessed=8 * width * columns,
            transcendentals=4 * (plan.halves - 1) * plan.block * columns,
        ),
        name="far_gradients",
    )(where, unit, turned, paired, first, second, factor, weights, raw, norm, before)


def join_kernel(*refs):
    out_ref = refs[-1]
    count, _, length = refs[0].shape
    columns = length - LANES
    start = 0
    for sender in range(count):
        for ref in refs[:-1]:
            factor = jnp.exp2(ref[sender, :, columns:])
            out_ref[:, start : start + columns] = ref[sender, :, :columns] * widen(factor, columns)
            start += columns


def join(pieces):
    senders, share, length = pieces[0].shape
    columns = (length - LANES) * len(pieces)
    each = tile_of(senders, 2)
    spec = pl.BlockSpec((each, share, length), lambda i: (i, 0, 0))
    return pl.pallas_call(
        join_kernel,
        out_shape=jax.ShapeDtypeStruct((share, senders * columns), F32),
        grid=(senders // each,),
        in_specs=[spec] * len(pieces),
        out_specs=pl.BlockSpec((share, each * columns), lambda i: (0, i)),
        compiler_params=params(16),
        cost_estimate=pl.CostEstimate(
            flops=share * senders * columns,
            bytes_accessed=8 * share * senders * columns,
            transcendentals=0,
        ),
        name="join",
    )(*pieces)


def swap(value, axis):
    return lax.ppermute(value, axis, [(0, 1), (1, 0)])


def exchange(value, axes):
    return lax.all_to_all(value, axes, split_axis=0, concat_axis=0, tiled=True)


def gather(value, axes, count):
    return exchange(jnp.tile(value, (count,) + (1,) * (value.ndim - 1)), axes)


def tie(value, *others):
    return lax.optimization_barrier((value,) + others)[0]


def body(teacher, students, prototypes, pairing, layout):
    halves, chips, protos = lax.axis_size("half"), lax.axis_size("chip"), lax.axis_size("protos")
    half, chip, core, proto = (lax.axis_index(a) for a in ("half", "chip", "core", "protos"))
    everyone = ("half", "chip", "core", "protos")
    all_chips = halves * chips
    width, held = prototypes.shape
    tea_count, stu_count = teacher.shape[0], students.shape[0]
    plan = Layout(halves, chips, protos, tea_count, stu_count)
    columns = held // (chips * 2)
    part_columns = columns // halves
    where = jnp.stack([half, chip, core]).astype(jnp.int32)
    parcel = lambda lanes: jax.ShapeDtypeStruct((plan.devices, lanes, LANES), F32)

    tea_own = gather(teacher, ("half", "chip"), all_chips)
    weights, flipped, norm, raw = unit_columns(where, prototypes, columns)
    near_total = local_denominator(tie(students, weights), prototypes, 0, 2)
    tea_own = tie(tea_own, near_total)
    tea_other = swap(tea_own, "core")
    parcel_one, tea_unit = sweep_call(
        first_sweep_kernel,
        plan,
        where,
        [tea_own, tea_other, weights, pairing.reshape(1, -1), layout.reshape(1, -1)],
        2,
        part_columns,
        [
            parcel(plan.tea_lanes + plan.stu_lanes),
            jax.ShapeDtypeStruct((2 * plan.tea_rows, width), BF16),
        ],
        "first_sweep",
    )
    first = exchange(parcel_one, everyone)
    far_total = local_denominator(tie(students, tea_unit), prototypes, 1, 2)

    markers = [weights, near_total, parcel_one]
    gathered = students[None]
    bit = all_chips // 2
    while bit:
        came = lax.ppermute(
            gathered, ("half", "chip"), [(q, q ^ bit) for q in range(all_chips)]
        )
        if markers:
            came = tie(came, markers.pop(0))
        gathered = jnp.concatenate([gathered, came], 0)
        bit //= 2
    stu_own = gathered.reshape(chips, halves, stu_count, width)
    stu_other = swap(stu_own, "core")

    parcel_two, factor = sweep_call(
        second_sweep_kernel,
        plan,
        where,
        [tea_unit, weights, first, near_total, far_total],
        1,
        part_columns,
        [
            parcel(plan.tea_lanes + plan.stu_lanes),
            jax.ShapeDtypeStruct((1, part_columns), F32),
        ],
        "second_sweep",
    )
    second = exchange(parcel_two, everyone)
    factors = [factor]
    for step in range(1, halves):
        factors.append(
            lax.ppermute(factor, "half", [(h, (h + step) % halves) for h in range(halves)])
        )
    if halves == 2:
        factors = [jnp.where(half == step, factors[0], factors[1]) for step in range(2)]
    elif halves > 2:
        factors = [jnp.stack(factors)[(half - step) % halves] for step in range(halves)]
    factor = jnp.concatenate(factors, 1)
    unit, turned, paired = pair(
        plan, where, stu_own, stu_other, tie(first, parcel_two), tea_unit
    )
    second, unit, turned, paired = lax.optimization_barrier((second, unit, turned, paired))

    rows_of = (unit, turned, paired, first, second, factor, weights)
    own_part, other_part, proto_all = near_gradients(
        plan, where, *rows_of, flipped, stu_own, stu_other
    )
    summed = (own_part + swap(other_part, "core")) * 128.0
    sent = summed.astype(F16).reshape(chips * protos, stu_count // protos, width)
    came = exchange(sent, ("chip", "protos"))
    rows = jnp.sum(came.astype(F32), 0) * (1.0 / 128.0)
    if protos == 2:
        far = swap(rows, "protos")
        grad_unit = jnp.concatenate(
            [jnp.where(proto == 0, rows, far), jnp.where(proto == 0, far, rows)], 0
        )
    else:
        grad_unit = gather(rows, "protos", protos)
    stu_full = students.astype(F32)
    u_norm = jnp.sqrt(jnp.sum(stu_full * stu_full, 1, keepdims=True) + epsilon)
    grad_students = grad_unit / u_norm

    share = width // (all_chips * 2)
    pieces = []
    proto_all = tie(proto_all, sent)
    for part in range(halves):
        proto_part = far_gradients(plan, where, part, *rows_of, raw, norm, proto_all)
        sent = proto_part.astype(F16).reshape(chips * 2, share, part_columns + LANES)
        sent = tie(sent, came)
        proto_all = tie(proto_all, sent)
        pieces.append(exchange(sent, ("chip", "core")).astype(F32))
    return (grad_students, join(pieces))


def solution(mesh):
    rows, protos = mesh.shape["rows"], mesh.shape["protos"]
    halves = HALVES
    split = Mesh(
        mesh.devices.reshape(halves, rows // (2 * halves), 2, protos),
        ("half", "chip", "core", "protos"),
    )
    over_rows = ("half", "chip", "core")
    in_specs = (
        P(over_rows, None),
        P(over_rows, None),
        P(None, "protos"),
        P(over_rows),
        P(over_rows),
    )
    out_specs = (P(over_rows, None), P(over_rows, "protos"))
    return jax.shard_map(
        body, mesh=split, in_specs=in_specs, out_specs=out_specs, check_vma=False
    )
```

```python
import functools

import jax
import jax.numpy as jnp
from jax import lax
from jax.experimental import pallas as pl
from jax.experimental.pallas import tpu as pltpu
from jax.sharding import Mesh, PartitionSpec as P

epsilon = 1e-06
teacher_temp = 0.07
student_temp = 0.1
loss_scale = 16.0

LOG2E = 1.4426950408889634
HALVES = 2
LANES = 128
MIB = 1024 * 1024
F32 = jnp.float32
BF16 = jnp.bfloat16
F16 = jnp.float16


def params(limit, grid=1):
    return pltpu.CompilerParams(
        vmem_limit_bytes=limit * MIB, dimension_semantics=("arbitrary",) * grid
    )


def tile_of(size, want):
    return want if size % want == 0 else size


def unit_rows(rows):
    full = rows.astype(F32)
    return full * (1.0 / jnp.sqrt(jnp.sum(full * full, 1, keepdims=True) + epsilon))


def lane_fold(block):
    total = block[:, :LANES]
    for start in range(LANES, block.shape[1], LANES):
        total = total + block[:, start : start + LANES]
    return total


def widen(column, width):
    return jnp.concatenate([column] * (width // LANES), 1)


def as_columns(values):
    return jnp.concatenate(
        [
            jnp.transpose(jnp.broadcast_to(values[i : i + 1], (LANES, LANES)))
            for i in range(values.shape[0])
        ],
        0,
    )


def as_rows(folded):
    return jnp.concatenate(
        [
            jnp.sum(jnp.transpose(folded[i : i + LANES]), 0, keepdims=True)
            for i in range(0, folded.shape[0], LANES)
        ],
        0,
    )


def dot(a, b):
    return jnp.dot(a, b, preferred_element_type=F32)


def reverse_bits(place, count):
    bits = count.bit_length() - 1
    return sum(((place >> i) & 1) << (bits - 1 - i) for i in range(bits))


class Layout:
    def __init__(self, halves, chips, protos, tea_count, stu_count):
        self.halves, self.chips, self.protos = halves, chips, protos
        self.devices = halves * chips * 2 * protos
        self.tea_rows = halves * chips * tea_count
        self.tea_lanes = 2 * self.tea_rows // LANES
        self.stu_lanes = stu_count // LANES
        self.stu_count = stu_count
        self.block = chips * stu_count

    def sender(self, where, other_half, other_core, place):
        half, chip, core = where[0], where[1], where[2]
        source = (half ^ other_half) * self.chips + (chip ^ reverse_bits(place, self.chips))
        return (source * 2 + (core ^ other_core)) * self.protos

    def teacher_totals(self, where, parcels_ref):
        sums = [None, None]
        for number in range(self.devices):
            side = (number // self.protos) % 2
            piece = parcels_ref[number, : self.tea_lanes]
            sums[side] = piece if sums[side] is None else sums[side] + piece
        cut = self.tea_lanes // 2
        turned = [jnp.concatenate([s[cut:], s[:cut]], 0) for s in sums]
        return jnp.where(where[2] == 0, sums[0] + turned[1], sums[1] + turned[0])


def columns_kernel(where_ref, raw_ref, unit_ref, flipped_ref, norm_ref, copy_ref):
    copy_ref[...] = raw_ref[...]
    full = raw_ref[...].astype(F32)
    norm = jnp.sqrt(jnp.sum(full * full, 0, keepdims=True) + epsilon)
    unit = full * (1.0 / norm)
    unit_ref[...] = unit.astype(BF16)
    flipped_ref[...] = jnp.transpose(unit.astype(BF16))
    norm_ref[...] = norm


def unit_columns(where, prototypes, columns):
    width = prototypes.shape[0]
    tile = tile_of(columns, 1024)
    steps = columns // tile
    return pl.pallas_call(
        columns_kernel,
        out_shape=[
            jax.ShapeDtypeStruct((width, columns), BF16),
            jax.ShapeDtypeStruct((columns, width), BF16),
            jax.ShapeDtypeStruct((1, columns), F32),
            jax.ShapeDtypeStruct((width, columns), BF16),
        ],
        grid_spec=pltpu.PrefetchScalarGridSpec(
            num_scalar_prefetch=1,
            grid=(steps,),
            in_specs=[
                pl.BlockSpec((width, tile), lambda j, w: (0, (w[1] * 2 + w[2]) * steps + j))
            ],
            out_specs=[
                pl.BlockSpec((width, tile), lambda j, w: (0, j)),
                pl.BlockSpec((tile, width), lambda j, w: (j, 0)),
                pl.BlockSpec((1, tile), lambda j, w: (0, j)),
                pl.BlockSpec((width, tile), lambda j, w: (0, j)),
            ],
        ),
        compiler_params=params(50),
        cost_estimate=pl.CostEstimate(
            flops=8 * width * columns, bytes_accessed=6 * width * columns, transcendentals=0
        ),
        name="unit_columns",
    )(where, prototypes)


def denominator_kernel(students_ref, weights_ref, total_ref, unit, folded, *, sub):
    step = pl.program_id(0)

    @pl.when(step == 0)
    def _():
        unit[...] = unit_rows(students_ref[...]).astype(BF16)
        folded[...] = jnp.zeros_like(folded)

    def scaled(start):
        weights = weights_ref[:, start : start + sub].astype(F32)
        inverse = 1.0 / jnp.sqrt(jnp.sum(weights * weights, 0, keepdims=True) + epsilon)
        return (weights * inverse).astype(BF16)

    total = folded[...]
    for start in range(0, weights_ref.shape[1], sub):
        logits = dot(unit[...], scaled(start))
        total = total + lane_fold(jnp.exp2(logits * (LOG2E / student_temp)))
    folded[...] = total

    @pl.when(step == pl.num_programs(0) - 1)
    def _():
        total_ref[...] = as_rows(folded[...])


def local_denominator(students, prototypes, part, parts):
    rows, width = students.shape
    columns = prototypes.shape[1] // parts
    tile = tile_of(columns, 4096)
    steps = columns // tile
    return pl.pallas_call(
        functools.partial(denominator_kernel, sub=tile_of(tile, 512)),
        out_shape=jax.ShapeDtypeStruct((rows // LANES, LANES), F32),
        grid=(steps,),
        in_specs=[
            pl.BlockSpec((rows, width), lambda j: (0, 0)),
            pl.BlockSpec((width, tile), lambda j: (0, part * steps + j)),
        ],
        out_specs=pl.BlockSpec((rows // LANES, LANES), lambda j: (0, 0)),
        scratch_shapes=[pltpu.VMEM((rows, width), BF16), pltpu.VMEM((rows, LANES), F32)],
        compiler_params=params(50),
        cost_estimate=pl.CostEstimate(
            flops=2 * rows * width * columns,
            bytes_accessed=2 * width * columns,
            transcendentals=rows * columns,
        ),
        name="denominator",
    )(students, prototypes)


def sweep_totals(units, weights_ref, column, sub, factor_ref):
    folded = jnp.zeros((units.shape[0], LANES), F32)
    for start in range(0, weights_ref.shape[1], sub):
        scores = jnp.exp2(dot(units, weights_ref[:, start : start + sub]) * (LOG2E / teacher_temp))
        weighted = scores if column is None else scores * widen(column, sub)
        factor = 1.0 / jnp.sum(weighted, 0, keepdims=True)
        if factor_ref is not None:
            factor_ref[:, start : start + sub] = factor
        folded = folded + lane_fold(scores * factor)
    return as_rows(folded)


def first_sweep_kernel(
    where_ref, own_ref, other_ref, weights_ref, pairing_ref, layout_ref, parcel_ref, unit_ref, mark_ref, *, plan, sub
):
    mark_ref[...] = jnp.zeros_like(mark_ref)
    half = own_ref.shape[0]
    unit_ref[:half, :] = unit_rows(own_ref[...]).astype(BF16)
    unit_ref[half:, :] = unit_rows(other_ref[...]).astype(BF16)
    totals = sweep_totals(unit_ref[...], weights_ref, None, sub, None)
    parcel_ref[:, : plan.tea_lanes, :] = jnp.broadcast_to(
        totals[None], (plan.devices,) + totals.shape
    )
    each = plan.tea_rows // (plan.halves * plan.chips)
    layout = layout_ref[...]
    index = (layout & 1) * half + (layout >> 1) * each + pairing_ref[...]
    index = index.astype(F32)
    for i in range(plan.stu_lanes):
        parcel_ref[:, plan.tea_lanes + i, :] = jnp.broadcast_to(
            index[:, i * LANES : (i + 1) * LANES], (plan.devices, LANES)
        )


def second_sweep_kernel(
    where_ref, unit_ref, weights_ref, came_ref, near_ref, far_ref, parcel_ref, factor_ref, *, plan, sub
):
    where = (where_ref[0], where_ref[1], where_ref[2])
    column = as_columns(1.0 / plan.teacher_totals(where, came_ref))
    totals = sweep_totals(unit_ref[...], weights_ref, column, sub, factor_ref)
    totals = jnp.concatenate([totals, near_ref[...] + far_ref[...]], 0)
    parcel_ref[...] = jnp.broadcast_to(totals[None], (plan.devices,) + totals.shape)


def sweep_call(kernel, plan, where, operands, weights_at, columns, out_shape, name):
    width = operands[0].shape[1]

    def spec(number, array):
        if number == weights_at:
            return pl.BlockSpec((width, columns), lambda i, w: (0, w[0]))
        return pl.BlockSpec(array.shape, lambda i, w: (0,) * len(array.shape))

    return pl.pallas_call(
        functools.partial(kernel, plan=plan, sub=tile_of(columns, 256)),
        out_shape=out_shape,
        grid_spec=pltpu.PrefetchScalarGridSpec(
            num_scalar_prefetch=1,
            grid=(1,),
            in_specs=[spec(i, a) for i, a in enumerate(operands)],
            out_specs=[
                pl.BlockSpec(o.shape, functools.partial(lambda n, i, w: (0,) * n, len(o.shape)))
                for o in out_shape
            ],
        ),
        compiler_params=params(16),
        cost_estimate=pl.CostEstimate(
            flops=4 * plan.tea_rows * width * columns,
            bytes_accessed=2 * width * (columns + 2 * plan.tea_rows),
            transcendentals=2 * plan.tea_rows * columns,
        ),
        name=name,
    )(where, *operands)


def pair_kernel(where_ref, own_ref, other_ref, came_ref, teacher_ref, unit_ref, turned_ref, paired_ref, mark_ref, *, plan):
    mark_ref[...] = jnp.zeros_like(mark_ref)
    where = (where_ref[0], where_ref[1], where_ref[2])
    apart = plan.halves - 1 - pl.program_id(0)
    teachers = teacher_ref.shape[0]
    count = plan.stu_count
    lane = lax.broadcasted_iota(jnp.int32, (count, LANES), 1).astype(F32)
    for side, ref in enumerate((own_ref, other_ref)):
        for place in range(plan.chips):
            rows = slice(place * count, (place + 1) * count)
            unit = unit_rows(ref[place, 0]).astype(BF16)
            unit_ref[0, side, rows, :] = unit
            turned_ref[0, side, :, rows] = jnp.transpose(unit)
            sender = plan.sender(where, apart, side, place)
            index = as_columns(came_ref[sender, plan.tea_lanes :, :])
            index = index + jnp.where(where[2] == 0, 0.0, float(teachers // 2))
            index = jnp.where(index >= teachers, index - teachers, index)
            chosen = jnp.concatenate(
                [
                    jnp.where(index == lane + start, 1.0, 0.0).astype(BF16)
                    for start in range(0, teachers, LANES)
                ],
                1,
            )
            paired_ref[0, side, rows, :] = dot(chosen, teacher_ref[...]).astype(BF16)


def pair(plan, where, own, other, came, teachers):
    width = own.shape[3]
    held = pl.BlockSpec(
        (plan.chips, 1, plan.stu_count, width), lambda g, w: (0, plan.halves - 1 - g, 0, 0)
    )
    rows = pl.BlockSpec((1, 2, plan.block, width), lambda g, w: (g, 0, 0, 0))
    return pl.pallas_call(
        functools.partial(pair_kernel, plan=plan),
        out_shape=[
            jax.ShapeDtypeStruct((plan.halves, 2, plan.block, width), BF16),
            jax.ShapeDtypeStruct((plan.halves, 2, width, plan.block), BF16),
            jax.ShapeDtypeStruct((plan.halves, 2, plan.block, width), BF16),
            jax.ShapeDtypeStruct((8, LANES), F32),
        ],
        grid_spec=pltpu.PrefetchScalarGridSpec(
            num_scalar_prefetch=1,
            grid=(plan.halves,),
            in_specs=[
                held,
                held,
                pl.BlockSpec(came.shape, lambda g, w: (0, 0, 0)),
                pl.BlockSpec(teachers.shape, lambda g, w: (0, 0)),
            ],
            out_specs=[
                rows,
                pl.BlockSpec((1, 2, width, plan.block), lambda g, w: (g, 0, 0, 0)),
                rows,
                pl.BlockSpec((8, LANES), lambda g, w: (0, 0)),
            ],
        ),
        compiler_params=params(50),
        cost_estimate=pl.CostEstimate(
            flops=4 * plan.halves * plan.block * width * teachers.shape[0],
            bytes_accessed=16 * plan.halves * plan.block * width,
            transcendentals=0,
        ),
        name="pair",
    )(where, own, other, came, teachers)


def fill_scale(plan, where, apart, side, first_ref, second_ref, row_factor, scale):
    teachers = plan.tea_lanes * LANES
    places = lax.broadcasted_iota(jnp.int32, (teachers, LANES), 0).astype(F32)
    own_first = jnp.where(where[2] == 0, 0.0, float(teachers // 2))
    for place in range(plan.chips):
        rows = slice(place * plan.stu_count, (place + 1) * plan.stu_count)
        sender = plan.sender(where, apart, side, place)
        total = second_ref[sender, plan.tea_lanes :, :]
        for proto in range(1, plan.protos):
            total = total + second_ref[sender + proto, plan.tea_lanes :, :]
        scale[0, rows, :] = as_columns((loss_scale / student_temp) / total)
        index = first_ref[sender, plan.tea_lanes :, :] + own_first
        index = jnp.where(index >= teachers, index - teachers, index)
        found = [
            jnp.sum(jnp.where(index[i : i + 1] == places, row_factor[...], 0.0), 0, keepdims=True)
            for i in range(plan.stu_lanes)
        ]
        scale[1, rows, :] = as_columns(jnp.concatenate(found, 0))


def gradient_products(
    unit_ref, turned_ref, paired_ref, factor_ref, weights_ref, flipped_ref, shares_ref, scale,
    grads, sub, earlier,
):
    columns = weights_ref.shape[1]
    tile = tile_of(columns, 4 * sub)

    def products(step, shares):
        base = pl.multiple_of(step * tile, tile)

        def logits(start):
            weights = weights_ref[:, pl.ds(base + start, sub)]
            return dot(unit_ref[0, 0], weights), dot(paired_ref[0, 0], weights)

        ahead = logits(0)
        for start in range(0, tile, sub):
            student, target = ahead
            if start + sub < tile:
                ahead = logits(start + sub)
            span = pl.ds(base + start, sub)
            student = jnp.exp2(student * (LOG2E / student_temp)) * widen(scale[0], sub)
            target = jnp.exp2(target * (LOG2E / teacher_temp)) * (
                widen(scale[1], sub) * factor_ref[:, span]
            )
            grad = (student - target).astype(BF16)
            if shares_ref is not None:
                share = dot(grad, flipped_ref[span, :])
                shares = share if shares is None else shares + share
            share = dot(turned_ref[0, 0], grad)
            grads[:, span] = earlier(span) + share
        return shares

    @pl.loop(0, columns // tile)
    def _(step):
        shares = products(step, None)
        if shares_ref is not None:
            shares_ref[...] += shares


def near_kernel(
    where_ref,
    unit_ref,
    turned_ref,
    paired_ref,
    first_ref,
    second_ref,
    factor_ref,
    weights_ref,
    flipped_ref,
    own_raw_ref,
    other_raw_ref,
    own_ref,
    other_ref,
    grads_ref,
    scale,
    shares,
    row_factor,
    *,
    plan,
    sub,
):
    where = (where_ref[0], where_ref[1], where_ref[2])
    part, side = pl.program_id(0), pl.program_id(1)
    count = plan.stu_count

    @pl.when((part == 0) & (side == 0))
    def _():
        row_factor[...] = as_columns(
            (loss_scale / student_temp) / plan.teacher_totals(where, second_ref)
        )

    @pl.when(part == 0)
    def _():
        fill_scale(plan, where, 0, side, first_ref, second_ref, row_factor, scale.at[side])
        shares[side] = jnp.zeros(shares.shape[1:], F32)

    gradient_products(
        unit_ref, turned_ref, paired_ref, factor_ref, weights_ref, flipped_ref, shares.at[side],
        scale.at[side], grads_ref, sub, lambda span: jnp.where(side == 0, 0.0, grads_ref[:, span]),
    )

    def finish(raw_ref, out_ref):
        for place in range(plan.chips):
            rows = slice(place * count, (place + 1) * count)
            chip = where[1] ^ reverse_bits(place, plan.chips)
            unit = unit_rows(raw_ref[place, 0])
            share = shares[side, rows, :]
            share = share - unit * jnp.sum(unit * share, 1, keepdims=True)
            out_ref[pl.ds(pl.multiple_of(chip * count, count), count), :] = share

    @pl.when((part == pl.num_programs(0) - 1) & (side == 0))
    def _():
        finish(own_raw_ref, own_ref)

    @pl.when((part == pl.num_programs(0) - 1) & (side == 1))
    def _():
        finish(other_raw_ref, other_ref)


def whole_spec(array):
    return pl.BlockSpec(
        array.shape, lambda q, p, w: (0,) * array.ndim, pipeline_mode=pl.Buffered(1)
    )


def parts_of(columns):
    return 2 if columns % (2 * LANES) == 0 else 1


def near_gradients(plan, where, unit, turned, paired, first, second, factor, weights, flipped, own, other):
    width, columns = weights.shape
    parts = parts_of(columns)
    each = columns // parts
    last = plan.halves - 1
    rows = pl.BlockSpec((1, 1, plan.block, width), lambda q, p, w: (last, p, 0, 0))
    across = pl.BlockSpec((width, each), lambda q, p, w: (0, q))
    raw = pl.BlockSpec(
        (plan.chips, 1, plan.stu_count, width),
        lambda q, p, w: (0, 0, 0, 0),
        pipeline_mode=pl.Buffered(1),
    )
    students = jax.ShapeDtypeStruct((plan.block, width), F32)
    return pl.pallas_call(
        functools.partial(near_kernel, plan=plan, sub=tile_of(each, 256)),
        out_shape=[students, students, jax.ShapeDtypeStruct((width, columns), F32)],
        grid_spec=pltpu.PrefetchScalarGridSpec(
            num_scalar_prefetch=1,
            grid=(parts, 2),
            in_specs=[
                rows,
                pl.BlockSpec((1, 1, width, plan.block), lambda q, p, w: (last, p, 0, 0)),
                rows,
                whole_spec(first),
                whole_spec(second),
                pl.BlockSpec((1, each), lambda q, p, w: (0, q)),
                across,
                pl.BlockSpec((each, width), lambda q, p, w: (q, 0)),
                raw,
                raw,
            ],
            out_specs=[whole_spec(students), whole_spec(students), across],
            scratch_shapes=[
                pltpu.VMEM((2, 2, plan.block, LANES), F32),
                pltpu.VMEM((2, plan.block, width), F32),
                pltpu.VMEM((plan.tea_lanes * LANES, LANES), F32),
            ],
        ),
        compiler_params=params(50, 2),
        cost_estimate=pl.CostEstimate(
            flops=16 * plan.block * width * columns,
            bytes_accessed=8 * width * columns,
            transcendentals=4 * plan.block * columns,
        ),
        name="near_gradients",
    )(where, unit, turned, paired, first, second, factor, weights, flipped, own, other)


def far_kernel(
    where_ref,
    unit_ref,
    turned_ref,
    paired_ref,
    first_ref,
    second_ref,
    factor_ref,
    weights_ref,
    raw_ref,
    norm_ref,
    before_ref,
    proto_ref,
    scale,
    grads,
    row_factor,
    *,
    plan,
    sub,
):
    where = (where_ref[0], where_ref[1], where_ref[2])
    part, block = pl.program_id(0), pl.program_id(1)
    columns = weights_ref.shape[1]

    @pl.when((part == 0) & (block == 0))
    def _():
        row_factor[...] = as_columns(
            (loss_scale / student_temp) / plan.teacher_totals(where, second_ref)
        )

    @pl.when(part == 0)
    def _():
        apart = plan.halves - 1 - block // 2
        fill_scale(
            plan, where, apart, block % 2, first_ref, second_ref, row_factor, scale.at[block]
        )

    gradient_products(
        unit_ref, turned_ref, paired_ref, factor_ref, weights_ref, None, None, scale.at[block],
        grads, sub, lambda span: jnp.where(block == 0, before_ref[:, span], grads[:, span]),
    )

    @pl.when(block == pl.num_programs(1) - 1)
    def _():
        kept = grads.shape[0] // plan.halves
        mine = pl.ds(pl.multiple_of(where[0] * kept, kept), kept)
        largest = jnp.zeros((kept, LANES), F32)
        for start in range(0, columns, sub):
            span = slice(start, start + sub)
            inverse = 1.0 / norm_ref[:, span]
            unit = raw_ref[:, span].astype(F32) * inverse
            along = jnp.sum(unit * grads[:, span], 0, keepdims=True)
            unit = raw_ref[mine, span].astype(F32) * inverse
            ready = (grads[mine, span] - unit * along) * inverse
            proto_ref[:, span] = ready
            ready = jnp.abs(ready)
            for i in range(0, sub, LANES):
                largest = jnp.maximum(largest, ready[:, i : i + LANES])
        largest = jnp.maximum(jnp.max(jnp.max(largest, 0, keepdims=True), 1, keepdims=True), 1e-30)
        power = jnp.floor(jnp.log2(largest)) - 13.0
        shrink = jnp.exp2(-power)
        for start in range(0, columns, sub):
            span = slice(start, start + sub)
            proto_ref[:, span] = proto_ref[:, span] * shrink
        proto_ref[:, columns:] = jnp.broadcast_to(power, (kept, LANES))


def far_gradients(
    plan, where, unit, turned, paired, first, second, factor, weights, raw, norm, before
):
    width, columns = weights.shape
    parts = parts_of(columns)
    each = columns // parts
    blocks = 2 * (plan.halves - 1)
    kept = width // plan.halves
    rows = pl.BlockSpec((1, 1, plan.block, width), lambda q, p, w: (p // 2, p % 2, 0, 0))
    across = pl.BlockSpec((width, each), lambda q, p, w: (0, q))
    thin = pl.BlockSpec((1, each), lambda q, p, w: (0, q))
    return pl.pallas_call(
        functools.partial(far_kernel, plan=plan, sub=tile_of(each, 256)),
        out_shape=jax.ShapeDtypeStruct((kept, parts * (each + LANES)), F32),
        grid_spec=pltpu.PrefetchScalarGridSpec(
            num_scalar_prefetch=1,
            grid=(parts, blocks),
            in_specs=[
                rows,
                pl.BlockSpec((1, 1, width, plan.block), lambda q, p, w: (p // 2, p % 2, 0, 0)),
                rows,
                whole_spec(first),
                whole_spec(second),
                thin,
                across,
                across,
                thin,
                across,
            ],
            out_specs=pl.BlockSpec((kept, each + LANES), lambda q, p, w: (0, q)),
            scratch_shapes=[
                pltpu.VMEM((blocks, 2, plan.block, LANES), F32),
                pltpu.VMEM((width, each), F32),
                pltpu.VMEM((plan.tea_lanes * LANES, LANES), F32),
            ],
        ),
        compiler_params=params(56, 2),
        cost_estimate=pl.CostEstimate(
            flops=12 * (plan.halves - 1) * plan.block * width * columns,
            bytes_accessed=8 * width * columns,
            transcendentals=4 * (plan.halves - 1) * plan.block * columns,
        ),
        name="far_gradients",
    )(where, unit, turned, paired, first, second, factor, weights, raw, norm, before)


def join_kernel(came_ref, out_ref, *, parts):
    count, _, length = came_ref.shape
    step = length // parts
    columns = step - LANES
    for number in range(count * parts):
        sender, start = number // parts, number % parts * step
        factor = jnp.exp2(came_ref[sender, :, start + columns : start + step])
        out_ref[:, number * columns : (number + 1) * columns] = came_ref[
            sender, :, start : start + columns
        ] * widen(factor, columns)


def join(came, parts):
    senders, share, length = came.shape
    columns = length - parts * LANES
    each = tile_of(senders, 2)
    return pl.pallas_call(
        functools.partial(join_kernel, parts=parts),
        out_shape=jax.ShapeDtypeStruct((share, senders * columns), F32),
        grid=(senders // each,),
        in_specs=[pl.BlockSpec((each, share, length), lambda i: (i, 0, 0))],
        out_specs=pl.BlockSpec((share, each * columns), lambda i: (0, i)),
        compiler_params=params(16),
        cost_estimate=pl.CostEstimate(
            flops=share * senders * columns,
            bytes_accessed=8 * share * senders * columns,
            transcendentals=0,
        ),
        name="join",
    )(came)


def swap(value, axis):
    return lax.ppermute(value, axis, [(0, 1), (1, 0)])


def exchange(value, axes):
    return lax.all_to_all(value, axes, split_axis=0, concat_axis=0, tiled=True)


def gather(value, axes, count):
    return exchange(jnp.tile(value, (count,) + (1,) * (value.ndim - 1)), axes)


def tie(value, *others):
    return lax.optimization_barrier((value,) + others)[0]


def body(teacher, students, prototypes, pairing, layout):
    halves, chips, protos = lax.axis_size("half"), lax.axis_size("chip"), lax.axis_size("protos")
    half, chip, core, proto = (lax.axis_index(a) for a in ("half", "chip", "core", "protos"))
    everyone = ("half", "chip", "core", "protos")
    all_chips = halves * chips
    width, held = prototypes.shape
    tea_count, stu_count = teacher.shape[0], students.shape[0]
    plan = Layout(halves, chips, protos, tea_count, stu_count)
    columns = held // (chips * 2)
    part_columns = columns // halves
    where = jnp.stack([half, chip, core]).astype(jnp.int32)
    parcel = lambda lanes: jax.ShapeDtypeStruct((plan.devices, lanes, LANES), F32)

    tea_own = gather(teacher, ("half", "chip"), all_chips)
    weights, flipped, norm, raw = unit_columns(where, prototypes, columns)
    near_total = local_denominator(tie(students, norm), prototypes, 0, 2)
    tea_other = swap(tea_own, "core")
    parcel_one, tea_unit, mark = sweep_call(
        first_sweep_kernel,
        plan,
        tie(where, near_total),
        [tea_own, tea_other, weights, pairing.reshape(1, -1), layout.reshape(1, -1)],
        2,
        part_columns,
        [
            parcel(plan.tea_lanes + plan.stu_lanes),
            jax.ShapeDtypeStruct((2 * plan.tea_rows, width), BF16),
            jax.ShapeDtypeStruct((8, LANES), F32),
        ],
        "first_sweep",
    )
    first = exchange(parcel_one, everyone)
    far_total = local_denominator(tie(students, mark), prototypes, 1, 2)

    markers = [norm, near_total, mark]
    gathered = students[None]
    bit = all_chips // 2
    while bit:
        came = lax.ppermute(
            gathered, ("half", "chip"), [(q, q ^ bit) for q in range(all_chips)]
        )
        if markers:
            came = tie(came, markers.pop(0))
        gathered = jnp.concatenate([gathered, came], 0)
        bit //= 2
    stu_own = gathered.reshape(chips, halves, stu_count, width)
    stu_other = swap(stu_own, "core")

    parcel_two, factor = sweep_call(
        second_sweep_kernel,
        plan,
        where,
        [tea_unit, weights, first, near_total, far_total],
        1,
        part_columns,
        [
            parcel(plan.tea_lanes + plan.stu_lanes),
            jax.ShapeDtypeStruct((1, part_columns), F32),
        ],
        "second_sweep",
    )
    second = exchange(parcel_two, everyone)
    unit, turned, paired, _ = pair(
        plan, where, stu_own, stu_other, tie(first, parcel_two), tea_unit
    )
    second, unit, turned, paired = lax.optimization_barrier((second, unit, turned, paired))
    factors = [factor]
    for step in range(1, halves):
        factors.append(
            lax.ppermute(factor, "half", [(h, (h + step) % halves) for h in range(halves)])
        )
    if halves == 2:
        factors = [jnp.where(half == step, factors[0], factors[1]) for step in range(2)]
    elif halves > 2:
        factors = [jnp.stack(factors)[(half - step) % halves] for step in range(halves)]
    factor = jnp.concatenate(factors, 1)

    rows_of = (unit, turned, paired, first, second, factor, weights)
    own_part, other_part, proto_all = near_gradients(
        plan, where, *rows_of, flipped, stu_own, stu_other
    )
    summed = (own_part + swap(other_part, "core")) * 128.0
    sent = summed.astype(F16).reshape(chips * protos, stu_count // protos, width)
    came = exchange(sent, ("chip", "protos"))
    proto_part = far_gradients(plan, tie(where, sent), *rows_of, raw, norm, proto_all)
    share = width // (all_chips * 2)
    sent = proto_part.astype(F16).reshape(chips * 2, share, -1)
    grad_protos = join(exchange(sent, ("chip", "core")).astype(F32), parts_of(columns))

    rows = jnp.sum(came.astype(F32), 0) * (1.0 / 128.0)
    if protos == 2:
        far = swap(rows, "protos")
        grad_unit = jnp.concatenate(
            [jnp.where(proto == 0, rows, far), jnp.where(proto == 0, far, rows)], 0
        )
    else:
        grad_unit = gather(rows, "protos", protos)
    stu_full = students.astype(F32)
    u_norm = jnp.sqrt(jnp.sum(stu_full * stu_full, 1, keepdims=True) + epsilon)
    return (grad_unit / u_norm, grad_protos)


def solution(mesh):
    rows, protos = mesh.shape["rows"], mesh.shape["protos"]
    halves = HALVES
    split = Mesh(
        mesh.devices.reshape(halves, rows // (2 * halves), 2, protos),
        ("half", "chip", "core", "protos"),
    )
    over_rows = ("half", "chip", "core")
    in_specs = (
        P(over_rows, None),
        P(over_rows, None),
        P(None, "protos"),
        P(over_rows),
        P(over_rows),
    )
    out_specs = (P(over_rows, None), P(over_rows, "protos"))
    return jax.shard_map(
        body, mesh=split, in_specs=in_specs, out_specs=out_specs, check_vma=False
    )
```

```python
import functools

import jax
import jax.numpy as jnp
from jax import lax
from jax.experimental import pallas as pl
from jax.experimental.pallas import tpu as pltpu
from jax.sharding import Mesh, PartitionSpec as P

epsilon = 1e-06
teacher_temp = 0.07
student_temp = 0.1
loss_scale = 16.0

LOG2E = 1.4426950408889634
HALVES = 2
LANES = 128
MIB = 1024 * 1024
F32 = jnp.float32
BF16 = jnp.bfloat16
F16 = jnp.float16


def params(limit, grid=1):
    return pltpu.CompilerParams(
        vmem_limit_bytes=limit * MIB, dimension_semantics=("arbitrary",) * grid
    )


def tile_of(size, want):
    return want if size % want == 0 else size


def unit_rows(rows):
    full = rows.astype(F32)
    return full * (1.0 / jnp.sqrt(jnp.sum(full * full, 1, keepdims=True) + epsilon))


def lane_fold(block):
    total = block[:, :LANES]
    for start in range(LANES, block.shape[1], LANES):
        total = total + block[:, start : start + LANES]
    return total


def widen(column, width):
    return jnp.concatenate([column] * (width // LANES), 1)


def as_columns(values):
    return jnp.concatenate(
        [
            jnp.transpose(jnp.broadcast_to(values[i : i + 1], (LANES, LANES)))
            for i in range(values.shape[0])
        ],
        0,
    )


def as_rows(folded):
    return jnp.concatenate(
        [
            jnp.sum(jnp.transpose(folded[i : i + LANES]), 0, keepdims=True)
            for i in range(0, folded.shape[0], LANES)
        ],
        0,
    )


def dot(a, b):
    return jnp.dot(a, b, preferred_element_type=F32)


def reverse_bits(place, count):
    bits = count.bit_length() - 1
    return sum(((place >> i) & 1) << (bits - 1 - i) for i in range(bits))


class Layout:
    def __init__(self, halves, chips, protos, tea_count, stu_count):
        self.halves, self.chips, self.protos = halves, chips, protos
        self.devices = halves * chips * 2 * protos
        self.tea_rows = halves * chips * tea_count
        self.tea_lanes = 2 * self.tea_rows // LANES
        self.stu_lanes = stu_count // LANES
        self.stu_count = stu_count
        self.block = chips * stu_count

    def sender(self, where, other_half, other_core, place):
        half, chip, core = where[0], where[1], where[2]
        source = (half ^ other_half) * self.chips + (chip ^ reverse_bits(place, self.chips))
        return (source * 2 + (core ^ other_core)) * self.protos

    def teacher_totals(self, where, parcels_ref):
        sums = [None, None]
        for number in range(self.devices):
            side = (number // self.protos) % 2
            piece = parcels_ref[number, : self.tea_lanes]
            sums[side] = piece if sums[side] is None else sums[side] + piece
        cut = self.tea_lanes // 2
        turned = [jnp.concatenate([s[cut:], s[:cut]], 0) for s in sums]
        return jnp.where(where[2] == 0, sums[0] + turned[1], sums[1] + turned[0])


def denominator_kernel(where_ref, students_ref, weights_ref, *refs, sub):
    total_ref, unit, folded = refs[-3:]
    step = pl.program_id(0)

    if len(refs) > 3:
        raw_ref, unit_ref, norm_ref = refs[:3]
        full = raw_ref[...].astype(F32)
        norm = jnp.sqrt(jnp.sum(full * full, 0, keepdims=True) + epsilon)
        unit_ref[...] = (full * (1.0 / norm)).astype(BF16)
        norm_ref[...] = norm

    @pl.when(step == 0)
    def _():
        unit[...] = unit_rows(students_ref[...]).astype(BF16)
        folded[...] = jnp.zeros_like(folded)

    def scaled(start):
        weights = weights_ref[:, start : start + sub].astype(F32)
        inverse = 1.0 / jnp.sqrt(jnp.sum(weights * weights, 0, keepdims=True) + epsilon)
        return (weights * inverse).astype(BF16)

    total = folded[...]
    for start in range(0, weights_ref.shape[1], sub):
        logits = dot(unit[...], scaled(start))
        total = total + lane_fold(jnp.exp2(logits * (LOG2E / student_temp)))
    folded[...] = total

    @pl.when(step == pl.num_programs(0) - 1)
    def _():
        total_ref[...] = as_rows(folded[...])


def local_denominator(where, students, prototypes, part, count, parts, mine=0):
    rows, width = students.shape
    columns = prototypes.shape[1] // parts
    tile = tile_of(columns, 4096)
    steps = columns // tile
    before = part * steps
    steps, columns = steps * count, columns * count
    in_specs = [
        pl.BlockSpec((rows, width), lambda j, w: (0, 0)),
        pl.BlockSpec((width, tile), lambda j, w: (0, before + j)),
    ]
    out_specs = [pl.BlockSpec((rows // LANES, LANES), lambda j, w: (0, 0))]
    out_shape = [jax.ShapeDtypeStruct((rows // LANES, LANES), F32)]
    operands = [students, prototypes]
    if mine:
        each = mine // steps
        operands.append(prototypes)
        in_specs.append(
            pl.BlockSpec((width, each), lambda j, w: (0, (w[1] * 2 + w[2]) * steps + j))
        )
        out_specs = [
            pl.BlockSpec((width, each), lambda j, w: (0, j)),
            pl.BlockSpec((1, each), lambda j, w: (0, j)),
        ] + out_specs
        out_shape = [
            jax.ShapeDtypeStruct((width, mine), BF16),
            jax.ShapeDtypeStruct((1, mine), F32),
        ] + out_shape
    return pl.pallas_call(
        functools.partial(denominator_kernel, sub=tile_of(tile, 512)),
        out_shape=out_shape,
        grid_spec=pltpu.PrefetchScalarGridSpec(
            num_scalar_prefetch=1,
            grid=(steps,),
            in_specs=in_specs,
            out_specs=out_specs,
            scratch_shapes=[pltpu.VMEM((rows, width), BF16), pltpu.VMEM((rows, LANES), F32)],
        ),
        compiler_params=params(50),
        cost_estimate=pl.CostEstimate(
            flops=2 * rows * width * columns,
            bytes_accessed=2 * width * columns,
            transcendentals=rows * columns,
        ),
        name="denominator",
    )(where, *operands)


def sweep_totals(units, weights_ref, column, sub, factor_ref):
    folded = jnp.zeros((units.shape[0], LANES), F32)
    for start in range(0, weights_ref.shape[1], sub):
        scores = jnp.exp2(dot(units, weights_ref[:, start : start + sub]) * (LOG2E / teacher_temp))
        weighted = scores if column is None else scores * widen(column, sub)
        factor = 1.0 / jnp.sum(weighted, 0, keepdims=True)
        if factor_ref is not None:
            factor_ref[:, start : start + sub] = factor
        folded = folded + lane_fold(scores * factor)
    return as_rows(folded)


def first_sweep_kernel(
    where_ref, own_ref, other_ref, weights_ref, pairing_ref, layout_ref, parcel_ref, unit_ref, mark_ref, *, plan, sub
):
    mark_ref[...] = jnp.zeros_like(mark_ref)
    half = own_ref.shape[0]
    unit_ref[:half, :] = unit_rows(own_ref[...]).astype(BF16)
    unit_ref[half:, :] = unit_rows(other_ref[...]).astype(BF16)
    totals = sweep_totals(unit_ref[...], weights_ref, None, sub, None)
    parcel_ref[:, : plan.tea_lanes, :] = jnp.broadcast_to(
        totals[None], (plan.devices,) + totals.shape
    )
    each = plan.tea_rows // (plan.halves * plan.chips)
    layout = layout_ref[...]
    index = (layout & 1) * half + (layout >> 1) * each + pairing_ref[...]
    index = index.astype(F32)
    for i in range(plan.stu_lanes):
        parcel_ref[:, plan.tea_lanes + i, :] = jnp.broadcast_to(
            index[:, i * LANES : (i + 1) * LANES], (plan.devices, LANES)
        )


def second_sweep_kernel(
    where_ref, unit_ref, weights_ref, came_ref, near_ref, far_ref, parcel_ref, factor_ref, *, plan, sub
):
    where = (where_ref[0], where_ref[1], where_ref[2])
    column = as_columns(1.0 / plan.teacher_totals(where, came_ref))
    totals = sweep_totals(unit_ref[...], weights_ref, column, sub, factor_ref)
    totals = jnp.concatenate([totals, near_ref[...] + far_ref[...]], 0)
    parcel_ref[...] = jnp.broadcast_to(totals[None], (plan.devices,) + totals.shape)


def sweep_call(kernel, plan, where, operands, weights_at, columns, out_shape, name):
    width = operands[0].shape[1]

    def spec(number, array):
        if number == weights_at:
            return pl.BlockSpec((width, columns), lambda i, w: (0, w[0]))
        return pl.BlockSpec(array.shape, lambda i, w: (0,) * len(array.shape))

    return pl.pallas_call(
        functools.partial(kernel, plan=plan, sub=tile_of(columns, 256)),
        out_shape=out_shape,
        grid_spec=pltpu.PrefetchScalarGridSpec(
            num_scalar_prefetch=1,
            grid=(1,),
            in_specs=[spec(i, a) for i, a in enumerate(operands)],
            out_specs=[
                pl.BlockSpec(o.shape, functools.partial(lambda n, i, w: (0,) * n, len(o.shape)))
                for o in out_shape
            ],
        ),
        compiler_params=params(16),
        cost_estimate=pl.CostEstimate(
            flops=4 * plan.tea_rows * width * columns,
            bytes_accessed=2 * width * (columns + 2 * plan.tea_rows),
            transcendentals=2 * plan.tea_rows * columns,
        ),
        name=name,
    )(where, *operands)


def pair_kernel(
    where_ref, own_ref, other_ref, came_ref, teacher_ref, weights_ref, both_ref, turned_ref,
    flipped_ref, *, plan
):
    where = (where_ref[0], where_ref[1], where_ref[2])
    apart = plan.halves - 1 - pl.program_id(0)
    teachers = teacher_ref.shape[0]
    count = plan.stu_count
    lane = lax.broadcasted_iota(jnp.int32, (count, LANES), 1).astype(F32)
    flipped_ref[...] = jnp.transpose(weights_ref[...])
    for side, ref in enumerate((own_ref, other_ref)):
        for place in range(plan.chips):
            rows = slice(place * count, (place + 1) * count)
            unit = unit_rows(ref[place, 0]).astype(BF16)
            both_ref[0, side, 0, rows, :] = unit
            turned_ref[0, side, :, rows] = jnp.transpose(unit)
            sender = plan.sender(where, apart, side, place)
            index = as_columns(came_ref[sender, plan.tea_lanes :, :])
            index = index + jnp.where(where[2] == 0, 0.0, float(teachers // 2))
            index = jnp.where(index >= teachers, index - teachers, index)
            chosen = jnp.concatenate(
                [
                    jnp.where(index == lane + start, 1.0, 0.0).astype(BF16)
                    for start in range(0, teachers, LANES)
                ],
                1,
            )
            both_ref[0, side, 1, rows, :] = dot(chosen, teacher_ref[...]).astype(BF16)


def pair(plan, where, own, other, came, teachers, weights):
    width, columns = weights.shape
    each = columns // plan.halves
    held = pl.BlockSpec(
        (plan.chips, 1, plan.stu_count, width), lambda g, w: (0, plan.halves - 1 - g, 0, 0)
    )
    return pl.pallas_call(
        functools.partial(pair_kernel, plan=plan),
        out_shape=[
            jax.ShapeDtypeStruct((plan.halves, 2, 2, plan.block, width), BF16),
            jax.ShapeDtypeStruct((plan.halves, 2, width, plan.block), BF16),
            jax.ShapeDtypeStruct((columns, width), BF16),
        ],
        grid_spec=pltpu.PrefetchScalarGridSpec(
            num_scalar_prefetch=1,
            grid=(plan.halves,),
            in_specs=[
                held,
                held,
                pl.BlockSpec(came.shape, lambda g, w: (0, 0, 0)),
                pl.BlockSpec(teachers.shape, lambda g, w: (0, 0)),
                pl.BlockSpec((width, each), lambda g, w: (0, g)),
            ],
            out_specs=[
                pl.BlockSpec((1, 2, 2, plan.block, width), lambda g, w: (g, 0, 0, 0, 0)),
                pl.BlockSpec((1, 2, width, plan.block), lambda g, w: (g, 0, 0, 0)),
                pl.BlockSpec((each, width), lambda g, w: (g, 0)),
            ],
        ),
        compiler_params=params(50),
        cost_estimate=pl.CostEstimate(
            flops=4 * plan.halves * plan.block * width * teachers.shape[0],
            bytes_accessed=16 * plan.halves * plan.block * width,
            transcendentals=0,
        ),
        name="pair",
    )(where, own, other, came, teachers, weights)


def fill_scale(plan, where, apart, side, first_ref, second_ref, row_factor, scale):
    teachers = plan.tea_lanes * LANES
    places = lax.broadcasted_iota(jnp.int32, (teachers, LANES), 0).astype(F32)
    own_first = jnp.where(where[2] == 0, 0.0, float(teachers // 2))
    for place in range(plan.chips):
        rows = slice(place * plan.stu_count, (place + 1) * plan.stu_count)
        sender = plan.sender(where, apart, side, place)
        total = second_ref[sender, plan.tea_lanes :, :]
        for proto in range(1, plan.protos):
            total = total + second_ref[sender + proto, plan.tea_lanes :, :]
        scale[0, rows, :] = as_columns((loss_scale / student_temp) / total)
        index = first_ref[sender, plan.tea_lanes :, :] + own_first
        index = jnp.where(index >= teachers, index - teachers, index)
        found = [
            jnp.sum(jnp.where(index[i : i + 1] == places, row_factor[...], 0.0), 0, keepdims=True)
            for i in range(plan.stu_lanes)
        ]
        scale[1, rows, :] = as_columns(jnp.concatenate(found, 0))


def gradient_products(
    both_ref, turned_ref, factor_ref, weights_ref, flipped_ref, shares_ref, scale, grads, sub,
    earlier,
):
    columns = weights_ref.shape[1]
    tile = tile_of(columns, 8 * sub)

    def products(step, shares):
        base = pl.multiple_of(step * tile, tile)

        def logits(start):
            weights = weights_ref[:, pl.ds(base + start, sub)]
            return dot(both_ref[0, 0, 0], weights), dot(both_ref[0, 0, 1], weights)

        ahead = logits(0)
        for start in range(0, tile, sub):
            student, target = ahead
            if start + sub < tile:
                ahead = logits(start + sub)
            span = pl.ds(base + start, sub)
            student = jnp.exp2(student * (LOG2E / student_temp)) * widen(scale[0], sub)
            target = jnp.exp2(target * (LOG2E / teacher_temp)) * (
                widen(scale[1], sub) * factor_ref[:, span]
            )
            grad = (student - target).astype(BF16)
            if shares_ref is not None:
                share = dot(grad, flipped_ref[span, :])
                shares = share if shares is None else shares + share
            share = dot(turned_ref[0, 0], grad)
            grads[:, span] = earlier(span) + share
        return shares

    @pl.loop(0, columns // tile)
    def _(step):
        shares = products(step, None)
        if shares_ref is not None:
            shares_ref[...] += shares


def near_kernel(
    where_ref,
    both_ref,
    turned_ref,
    first_ref,
    second_ref,
    factor_ref,
    weights_ref,
    flipped_ref,
    own_raw_ref,
    other_raw_ref,
    own_ref,
    other_ref,
    grads_ref,
    scale,
    shares,
    row_factor,
    *,
    plan,
    sub,
):
    where = (where_ref[0], where_ref[1], where_ref[2])
    part, side = pl.program_id(0), pl.program_id(1)
    count = plan.stu_count

    @pl.when((part == 0) & (side == 0))
    def _():
        row_factor[...] = as_columns(
            (loss_scale / student_temp) / plan.teacher_totals(where, second_ref)
        )

    @pl.when(part == 0)
    def _():
        fill_scale(plan, where, 0, side, first_ref, second_ref, row_factor, scale.at[side])
        shares[side] = jnp.zeros(shares.shape[1:], F32)

    gradient_products(
        both_ref, turned_ref, factor_ref, weights_ref, flipped_ref, shares.at[side],
        scale.at[side], grads_ref, sub, lambda span: jnp.where(side == 0, 0.0, grads_ref[:, span]),
    )

    def finish(raw_ref, out_ref):
        for place in range(plan.chips):
            rows = slice(place * count, (place + 1) * count)
            chip = where[1] ^ reverse_bits(place, plan.chips)
            unit = unit_rows(raw_ref[place, 0])
            share = shares[side, rows, :]
            share = share - unit * jnp.sum(unit * share, 1, keepdims=True)
            out_ref[pl.ds(pl.multiple_of(chip * count, count), count), :] = share

    @pl.when((part == pl.num_programs(0) - 1) & (side == 0))
    def _():
        finish(own_raw_ref, own_ref)

    @pl.when((part == pl.num_programs(0) - 1) & (side == 1))
    def _():
        finish(other_raw_ref, other_ref)


def whole_spec(array):
    return pl.BlockSpec(
        array.shape, lambda q, p, w: (0,) * array.ndim, pipeline_mode=pl.Buffered(1)
    )


def parts_of(columns):
    return 2 if columns % (2 * LANES) == 0 else 1


def near_gradients(plan, where, both, turned, first, second, factor, weights, flipped, own, other):
    width, columns = weights.shape
    parts = parts_of(columns)
    each = columns // parts
    last = plan.halves - 1
    rows = pl.BlockSpec((1, 1, 2, plan.block, width), lambda q, p, w: (last, p, 0, 0, 0))
    across = pl.BlockSpec((width, each), lambda q, p, w: (0, q))
    raw = pl.BlockSpec(
        (plan.chips, 1, plan.stu_count, width),
        lambda q, p, w: (0, 0, 0, 0),
        pipeline_mode=pl.Buffered(1),
    )
    students = jax.ShapeDtypeStruct((plan.block, width), F32)
    return pl.pallas_call(
        functools.partial(near_kernel, plan=plan, sub=tile_of(each, 256)),
        out_shape=[students, students, jax.ShapeDtypeStruct((width, columns), F32)],
        grid_spec=pltpu.PrefetchScalarGridSpec(
            num_scalar_prefetch=1,
            grid=(parts, 2),
            in_specs=[
                rows,
                pl.BlockSpec((1, 1, width, plan.block), lambda q, p, w: (last, p, 0, 0)),
                whole_spec(first),
                whole_spec(second),
                pl.BlockSpec((1, each), lambda q, p, w: (0, q)),
                across,
                pl.BlockSpec((each, width), lambda q, p, w: (q, 0)),
                raw,
                raw,
            ],
            out_specs=[whole_spec(students), whole_spec(students), across],
            scratch_shapes=[
                pltpu.VMEM((2, 2, plan.block, LANES), F32),
                pltpu.VMEM((2, plan.block, width), F32),
                pltpu.VMEM((plan.tea_lanes * LANES, LANES), F32),
            ],
        ),
        compiler_params=params(50, 2),
        cost_estimate=pl.CostEstimate(
            flops=16 * plan.block * width * columns,
            bytes_accessed=8 * width * columns,
            transcendentals=4 * plan.block * columns,
        ),
        name="near_gradients",
    )(where, both, turned, first, second, factor, weights, flipped, own, other)


def far_kernel(
    where_ref,
    both_ref,
    turned_ref,
    first_ref,
    second_ref,
    factor_ref,
    weights_ref,
    raw_ref,
    norm_ref,
    before_ref,
    proto_ref,
    scale,
    grads,
    row_factor,
    *,
    plan,
    sub,
):
    where = (where_ref[0], where_ref[1], where_ref[2])
    part, block = pl.program_id(0), pl.program_id(1)
    columns = weights_ref.shape[1]

    @pl.when((part == 0) & (block == 0))
    def _():
        row_factor[...] = as_columns(
            (loss_scale / student_temp) / plan.teacher_totals(where, second_ref)
        )

    @pl.when(part == 0)
    def _():
        apart = plan.halves - 1 - block // 2
        fill_scale(
            plan, where, apart, block % 2, first_ref, second_ref, row_factor, scale.at[block]
        )

    gradient_products(
        both_ref, turned_ref, factor_ref, weights_ref, None, None, scale.at[block],
        grads, sub, lambda span: jnp.where(block == 0, before_ref[:, span], grads[:, span]),
    )

    @pl.when(block == pl.num_programs(1) - 1)
    def _():
        kept = grads.shape[0] // plan.halves
        mine = pl.ds(pl.multiple_of(where[0] * kept, kept), kept)
        largest = jnp.zeros((kept, LANES), F32)
        for start in range(0, columns, sub):
            span = slice(start, start + sub)
            inverse = 1.0 / norm_ref[:, span]
            unit = raw_ref[:, span].astype(F32) * inverse
            along = jnp.sum(unit * grads[:, span], 0, keepdims=True)
            unit = raw_ref[mine, span].astype(F32) * inverse
            ready = (grads[mine, span] - unit * along) * inverse
            proto_ref[:, span] = ready
            ready = jnp.abs(ready)
            for i in range(0, sub, LANES):
                largest = jnp.maximum(largest, ready[:, i : i + LANES])
        largest = jnp.maximum(jnp.max(jnp.max(largest, 0, keepdims=True), 1, keepdims=True), 1e-30)
        power = jnp.floor(jnp.log2(largest)) - 13.0
        shrink = jnp.exp2(-power)
        for start in range(0, columns, sub):
            span = slice(start, start + sub)
            proto_ref[:, span] = proto_ref[:, span] * shrink
        proto_ref[:, columns:] = jnp.broadcast_to(power, (kept, LANES))


def far_gradients(
    plan, where, both, turned, first, second, factor, weights, prototypes, norm, before
):
    width, columns = weights.shape
    parts = parts_of(columns)
    each = columns // parts
    blocks = 2 * (plan.halves - 1)
    kept = width // plan.halves
    rows = pl.BlockSpec((1, 1, 2, plan.block, width), lambda q, p, w: (p // 2, p % 2, 0, 0, 0))
    across = pl.BlockSpec((width, each), lambda q, p, w: (0, q))
    thin = pl.BlockSpec((1, each), lambda q, p, w: (0, q))
    return pl.pallas_call(
        functools.partial(far_kernel, plan=plan, sub=tile_of(each, 256)),
        out_shape=jax.ShapeDtypeStruct((kept, parts * (each + LANES)), F32),
        grid_spec=pltpu.PrefetchScalarGridSpec(
            num_scalar_prefetch=1,
            grid=(parts, blocks),
            in_specs=[
                rows,
                pl.BlockSpec((1, 1, width, plan.block), lambda q, p, w: (p // 2, p % 2, 0, 0)),
                whole_spec(first),
                whole_spec(second),
                thin,
                across,
                pl.BlockSpec((width, each), lambda q, p, w: (0, (w[1] * 2 + w[2]) * parts + q)),
                thin,
                across,
            ],
            out_specs=pl.BlockSpec((kept, each + LANES), lambda q, p, w: (0, q)),
            scratch_shapes=[
                pltpu.VMEM((blocks, 2, plan.block, LANES), F32),
                pltpu.VMEM((width, each), F32),
                pltpu.VMEM((plan.tea_lanes * LANES, LANES), F32),
            ],
        ),
        compiler_params=params(46, 2),
        cost_estimate=pl.CostEstimate(
            flops=12 * (plan.halves - 1) * plan.block * width * columns,
            bytes_accessed=8 * width * columns,
            transcendentals=4 * (plan.halves - 1) * plan.block * columns,
        ),
        name="far_gradients",
    )(where, both, turned, first, second, factor, weights, prototypes, norm, before)


def join_kernel(came_ref, out_ref, *, parts):
    count, _, length = came_ref.shape
    step = length // parts
    columns = step - LANES
    for number in range(count * parts):
        sender, start = number // parts, number % parts * step
        factor = jnp.exp2(came_ref[sender, :, start + columns : start + step])
        out_ref[:, number * columns : (number + 1) * columns] = came_ref[
            sender, :, start : start + columns
        ] * widen(factor, columns)


def join(came, parts):
    senders, share, length = came.shape
    columns = length - parts * LANES
    each = tile_of(senders, 2)
    return pl.pallas_call(
        functools.partial(join_kernel, parts=parts),
        out_shape=jax.ShapeDtypeStruct((share, senders * columns), F32),
        grid=(senders // each,),
        in_specs=[pl.BlockSpec((each, share, length), lambda i: (i, 0, 0))],
        out_specs=pl.BlockSpec((share, each * columns), lambda i: (0, i)),
        compiler_params=params(16),
        cost_estimate=pl.CostEstimate(
            flops=share * senders * columns,
            bytes_accessed=8 * share * senders * columns,
            transcendentals=0,
        ),
        name="join",
    )(came)


def swap(value, axis):
    return lax.ppermute(value, axis, [(0, 1), (1, 0)])


def exchange(value, axes):
    return lax.all_to_all(value, axes, split_axis=0, concat_axis=0, tiled=True)


def gather(value, axes, count):
    return exchange(jnp.tile(value, (count,) + (1,) * (value.ndim - 1)), axes)


def tie(value, *others):
    return lax.optimization_barrier((value,) + others)[0]


def body(teacher, students, prototypes, pairing, layout):
    halves, chips, protos = lax.axis_size("half"), lax.axis_size("chip"), lax.axis_size("protos")
    half, chip, core, proto = (lax.axis_index(a) for a in ("half", "chip", "core", "protos"))
    everyone = ("half", "chip", "core", "protos")
    all_chips = halves * chips
    width, held = prototypes.shape
    tea_count, stu_count = teacher.shape[0], students.shape[0]
    plan = Layout(halves, chips, protos, tea_count, stu_count)
    columns = held // (chips * 2)
    part_columns = columns // halves
    where = jnp.stack([half, chip, core]).astype(jnp.int32)
    parcel = lambda lanes: jax.ShapeDtypeStruct((plan.devices, lanes, LANES), F32)

    tiled = jnp.tile(teacher, (all_chips, 1))
    tea_own = exchange(tiled, ("half", "chip"))
    weights, norm, near_total = local_denominator(
        tie(where, tiled), students, prototypes, 0, 1, 4, columns
    )
    tea_other = swap(tea_own, "core")
    parcel_one, tea_unit, mark = sweep_call(
        first_sweep_kernel,
        plan,
        tie(where, near_total),
        [tea_own, tea_other, weights, pairing.reshape(1, -1), layout.reshape(1, -1)],
        2,
        part_columns,
        [
            parcel(plan.tea_lanes + plan.stu_lanes),
            jax.ShapeDtypeStruct((2 * plan.tea_rows, width), BF16),
            jax.ShapeDtypeStruct((8, LANES), F32),
        ],
        "first_sweep",
    )
    first = exchange(parcel_one, everyone)
    (far_total,) = local_denominator(tie(where, mark), students, prototypes, 1, 3, 4)

    markers = [near_total, mark, far_total]
    gathered = tie(students, tiled)[None]
    bit = all_chips // 2
    while bit:
        came = lax.ppermute(
            gathered, ("half", "chip"), [(q, q ^ bit) for q in range(all_chips)]
        )
        if markers:
            came = tie(came, markers.pop(0))
        gathered = jnp.concatenate([gathered, came], 0)
        bit //= 2
    stu_own = gathered.reshape(chips, halves, stu_count, width)
    stu_other = swap(stu_own, "core")

    parcel_two, factor = sweep_call(
        second_sweep_kernel,
        plan,
        where,
        [tea_unit, weights, first, near_total, far_total],
        1,
        part_columns,
        [
            parcel(plan.tea_lanes + plan.stu_lanes),
            jax.ShapeDtypeStruct((1, part_columns), F32),
        ],
        "second_sweep",
    )
    second = exchange(parcel_two, everyone)
    both, turned, flipped = pair(
        plan, where, stu_own, stu_other, tie(first, parcel_two), tea_unit, weights
    )
    second, both, turned, flipped = lax.optimization_barrier((second, both, turned, flipped))
    factors = [factor]
    for step in range(1, halves):
        factors.append(
            lax.ppermute(factor, "half", [(h, (h + step) % halves) for h in range(halves)])
        )
    if halves == 2:
        factors = [jnp.where(half == step, factors[0], factors[1]) for step in range(2)]
    elif halves > 2:
        factors = [jnp.stack(factors)[(half - step) % halves] for step in range(halves)]
    factor = jnp.concatenate(factors, 1)

    rows_of = (both, turned, first, second, factor, weights)
    own_part, other_part, proto_all = near_gradients(
        plan, where, *rows_of, flipped, stu_own, stu_other
    )
    summed = (own_part + swap(other_part, "core")) * 128.0
    sent = summed.astype(F16).reshape(chips * protos, stu_count // protos, width)
    came = exchange(sent, ("chip", "protos"))
    proto_part = far_gradients(plan, tie(where, sent), *rows_of, prototypes, norm, proto_all)
    share = width // (all_chips * 2)
    sent = proto_part.astype(F16).reshape(chips * 2, share, -1)
    grad_protos = join(exchange(sent, ("chip", "core")).astype(F32), parts_of(columns))

    rows = jnp.sum(came.astype(F32), 0) * (1.0 / 128.0)
    if protos == 2:
        far = swap(rows, "protos")
        grad_unit = jnp.concatenate(
            [jnp.where(proto == 0, rows, far), jnp.where(proto == 0, far, rows)], 0
        )
    else:
        grad_unit = gather(rows, "protos", protos)
    stu_full = students.astype(F32)
    u_norm = jnp.sqrt(jnp.sum(stu_full * stu_full, 1, keepdims=True) + epsilon)
    return (grad_unit / u_norm, grad_protos)


def solution(mesh):
    rows, protos = mesh.shape["rows"], mesh.shape["protos"]
    halves = HALVES
    split = Mesh(
        mesh.devices.reshape(halves, rows // (2 * halves), 2, protos),
        ("half", "chip", "core", "protos"),
    )
    over_rows = ("half", "chip", "core")
    in_specs = (
        P(over_rows, None),
        P(over_rows, None),
        P(None, "protos"),
        P(over_rows),
        P(over_rows),
    )
    out_specs = (P(over_rows, None), P(over_rows, "protos"))
    return jax.shard_map(
        body, mesh=split, in_specs=in_specs, out_specs=out_specs, check_vma=False
    )
```

```python
import functools

import jax
import jax.numpy as jnp
from jax import lax
from jax.experimental import pallas as pl
from jax.experimental.pallas import tpu as pltpu
from jax.sharding import Mesh, PartitionSpec as P

epsilon = 1e-06
teacher_temp = 0.07
student_temp = 0.1
loss_scale = 16.0

LOG2E = 1.4426950408889634
HALVES = 2
LANES = 128
MIB = 1024 * 1024
F32 = jnp.float32
BF16 = jnp.bfloat16
F16 = jnp.float16


def params(limit, grid=1):
    return pltpu.CompilerParams(
        vmem_limit_bytes=limit * MIB, dimension_semantics=("arbitrary",) * grid
    )


def tile_of(size, want):
    return want if size % want == 0 else size


def unit_rows(rows):
    full = rows.astype(F32)
    return full * (1.0 / jnp.sqrt(jnp.sum(full * full, 1, keepdims=True) + epsilon))


def lane_fold(block):
    total = block[:, :LANES]
    for start in range(LANES, block.shape[1], LANES):
        total = total + block[:, start : start + LANES]
    return total


def widen(column, width):
    return jnp.concatenate([column] * (width // LANES), 1)


def as_columns(values):
    return jnp.concatenate(
        [
            jnp.transpose(jnp.broadcast_to(values[i : i + 1], (LANES, LANES)))
            for i in range(values.shape[0])
        ],
        0,
    )


def as_rows(folded):
    return jnp.concatenate(
        [
            jnp.sum(jnp.transpose(folded[i : i + LANES]), 0, keepdims=True)
            for i in range(0, folded.shape[0], LANES)
        ],
        0,
    )


def dot(a, b):
    return jnp.dot(a, b, preferred_element_type=F32)


def reverse_bits(place, count):
    bits = count.bit_length() - 1
    return sum(((place >> i) & 1) << (bits - 1 - i) for i in range(bits))


class Layout:
    def __init__(self, halves, chips, protos, tea_count, stu_count):
        self.halves, self.chips, self.protos = halves, chips, protos
        self.devices = halves * chips * 2 * protos
        self.tea_rows = halves * chips * tea_count
        self.tea_lanes = 2 * self.tea_rows // LANES
        self.stu_lanes = stu_count // LANES
        self.stu_count = stu_count
        self.block = chips * stu_count

    def sender(self, where, other_half, other_core, place):
        half, chip, core = where[0], where[1], where[2]
        source = (half ^ other_half) * self.chips + (chip ^ reverse_bits(place, self.chips))
        return (source * 2 + (core ^ other_core)) * self.protos

    def teacher_totals(self, where, parcels_ref):
        sums = [None, None]
        for number in range(self.devices):
            side = (number // self.protos) % 2
            piece = parcels_ref[number, : self.tea_lanes]
            sums[side] = piece if sums[side] is None else sums[side] + piece
        cut = self.tea_lanes // 2
        turned = [jnp.concatenate([s[cut:], s[:cut]], 0) for s in sums]
        return jnp.where(where[2] == 0, sums[0] + turned[1], sums[1] + turned[0])


def denominator_kernel(where_ref, students_ref, weights_ref, *refs, sub):
    total_ref, unit, folded = refs[-3:]
    step = pl.program_id(0)

    if len(refs) > 3:
        raw_ref, unit_ref, norm_ref = refs[:3]
        full = raw_ref[...].astype(F32)
        norm = jnp.sqrt(jnp.sum(full * full, 0, keepdims=True) + epsilon)
        unit_ref[...] = (full * (1.0 / norm)).astype(BF16)
        norm_ref[...] = norm

    @pl.when(step == 0)
    def _():
        unit[...] = unit_rows(students_ref[...]).astype(BF16)
        folded[...] = jnp.zeros_like(folded)

    def scaled(start):
        weights = weights_ref[:, start : start + sub].astype(F32)
        inverse = 1.0 / jnp.sqrt(jnp.sum(weights * weights, 0, keepdims=True) + epsilon)
        return (weights * inverse).astype(BF16)

    total = folded[...]
    for start in range(0, weights_ref.shape[1], sub):
        logits = dot(unit[...], scaled(start))
        total = total + lane_fold(jnp.exp2(logits * (LOG2E / student_temp)))
    folded[...] = total

    @pl.when(step == pl.num_programs(0) - 1)
    def _():
        total_ref[...] = as_rows(folded[...])


def local_denominator(where, students, prototypes, part, count, parts, mine=0):
    rows, width = students.shape
    columns = prototypes.shape[1] // parts
    tile = tile_of(columns, 4096)
    steps = columns // tile
    before = part * steps
    steps, columns = steps * count, columns * count
    in_specs = [
        pl.BlockSpec((rows, width), lambda j, w: (0, 0)),
        pl.BlockSpec((width, tile), lambda j, w: (0, before + j)),
    ]
    out_specs = [pl.BlockSpec((rows // LANES, LANES), lambda j, w: (0, 0))]
    out_shape = [jax.ShapeDtypeStruct((rows // LANES, LANES), F32)]
    operands = [students, prototypes]
    if mine:
        each = mine // steps
        operands.append(prototypes)
        in_specs.append(
            pl.BlockSpec((width, each), lambda j, w: (0, (w[1] * 2 + w[2]) * steps + j))
        )
        out_specs = [
            pl.BlockSpec((width, each), lambda j, w: (0, j)),
            pl.BlockSpec((1, each), lambda j, w: (0, j)),
        ] + out_specs
        out_shape = [
            jax.ShapeDtypeStruct((width, mine), BF16),
            jax.ShapeDtypeStruct((1, mine), F32),
        ] + out_shape
    return pl.pallas_call(
        functools.partial(denominator_kernel, sub=tile_of(tile, 512)),
        out_shape=out_shape,
        grid_spec=pltpu.PrefetchScalarGridSpec(
            num_scalar_prefetch=1,
            grid=(steps,),
            in_specs=in_specs,
            out_specs=out_specs,
            scratch_shapes=[pltpu.VMEM((rows, width), BF16), pltpu.VMEM((rows, LANES), F32)],
        ),
        compiler_params=params(50),
        cost_estimate=pl.CostEstimate(
            flops=2 * rows * width * columns,
            bytes_accessed=2 * width * columns,
            transcendentals=rows * columns,
        ),
        name="denominator",
    )(where, *operands)


def sweep_totals(units, weights_ref, column, sub, factor_ref):
    folded = jnp.zeros((units.shape[0], LANES), F32)
    for start in range(0, weights_ref.shape[1], sub):
        scores = jnp.exp2(dot(units, weights_ref[:, start : start + sub]) * (LOG2E / teacher_temp))
        weighted = scores if column is None else scores * widen(column, sub)
        factor = 1.0 / jnp.sum(weighted, 0, keepdims=True)
        if factor_ref is not None:
            factor_ref[:, start : start + sub] = factor
        folded = folded + lane_fold(scores * factor)
    return as_rows(folded)


def first_sweep_kernel(
    where_ref, own_ref, other_ref, weights_ref, pairing_ref, layout_ref, parcel_ref, unit_ref, mark_ref, *, plan, sub
):
    mark_ref[...] = jnp.zeros_like(mark_ref)
    half = own_ref.shape[0]
    unit_ref[:half, :] = unit_rows(own_ref[...]).astype(BF16)
    unit_ref[half:, :] = unit_rows(other_ref[...]).astype(BF16)
    totals = sweep_totals(unit_ref[...], weights_ref, None, sub, None)
    parcel_ref[:, : plan.tea_lanes, :] = jnp.broadcast_to(
        totals[None], (plan.devices,) + totals.shape
    )
    each = plan.tea_rows // (plan.halves * plan.chips)
    layout = layout_ref[...]
    index = (layout & 1) * half + (layout >> 1) * each + pairing_ref[...]
    index = index.astype(F32)
    for i in range(plan.stu_lanes):
        parcel_ref[:, plan.tea_lanes + i, :] = jnp.broadcast_to(
            index[:, i * LANES : (i + 1) * LANES], (plan.devices, LANES)
        )


def second_sweep_kernel(
    where_ref, unit_ref, weights_ref, came_ref, near_ref, far_ref, parcel_ref, factor_ref, *, plan, sub
):
    where = (where_ref[0], where_ref[1], where_ref[2])
    column = as_columns(1.0 / plan.teacher_totals(where, came_ref))
    totals = sweep_totals(unit_ref[...], weights_ref, column, sub, factor_ref)
    totals = jnp.concatenate([totals, near_ref[...] + far_ref[...]], 0)
    parcel_ref[...] = jnp.broadcast_to(totals[None], (plan.devices,) + totals.shape)


def sweep_call(kernel, plan, where, operands, weights_at, columns, out_shape, name):
    width = operands[0].shape[1]

    def spec(number, array):
        if number == weights_at:
            return pl.BlockSpec((width, columns), lambda i, w: (0, w[0]))
        return pl.BlockSpec(array.shape, lambda i, w: (0,) * len(array.shape))

    return pl.pallas_call(
        functools.partial(kernel, plan=plan, sub=tile_of(columns, 256)),
        out_shape=out_shape,
        grid_spec=pltpu.PrefetchScalarGridSpec(
            num_scalar_prefetch=1,
            grid=(1,),
            in_specs=[spec(i, a) for i, a in enumerate(operands)],
            out_specs=[
                pl.BlockSpec(o.shape, functools.partial(lambda n, i, w: (0,) * n, len(o.shape)))
                for o in out_shape
            ],
        ),
        compiler_params=params(16),
        cost_estimate=pl.CostEstimate(
            flops=4 * plan.tea_rows * width * columns,
            bytes_accessed=2 * width * (columns + 2 * plan.tea_rows),
            transcendentals=2 * plan.tea_rows * columns,
        ),
        name=name,
    )(where, *operands)


def pair_kernel(
    where_ref, own_ref, other_ref, came_ref, teacher_ref, weights_ref, both_ref, turned_ref,
    flipped_ref, *, plan
):
    where = (where_ref[0], where_ref[1], where_ref[2])
    apart = plan.halves - 1 - pl.program_id(0)
    teachers = teacher_ref.shape[0]
    count = plan.stu_count
    lane = lax.broadcasted_iota(jnp.int32, (count, LANES), 1).astype(F32)
    flipped_ref[...] = jnp.transpose(weights_ref[...])
    for side, ref in enumerate((own_ref, other_ref)):
        for place in range(plan.chips):
            rows = slice(place * count, (place + 1) * count)
            unit = unit_rows(ref[place, 0]).astype(BF16)
            both_ref[0, side, 0, rows, :] = unit
            turned_ref[0, side, :, rows] = jnp.transpose(unit)
            sender = plan.sender(where, apart, side, place)
            index = as_columns(came_ref[sender, plan.tea_lanes :, :])
            index = index + jnp.where(where[2] == 0, 0.0, float(teachers // 2))
            index = jnp.where(index >= teachers, index - teachers, index)
            chosen = jnp.concatenate(
                [
                    jnp.where(index == lane + start, 1.0, 0.0).astype(BF16)
                    for start in range(0, teachers, LANES)
                ],
                1,
            )
            both_ref[0, side, 1, rows, :] = dot(chosen, teacher_ref[...]).astype(BF16)


def pair(plan, where, own, other, came, teachers, weights):
    width, columns = weights.shape
    each = columns // plan.halves
    held = pl.BlockSpec(
        (plan.chips, 1, plan.stu_count, width), lambda g, w: (0, plan.halves - 1 - g, 0, 0)
    )
    return pl.pallas_call(
        functools.partial(pair_kernel, plan=plan),
        out_shape=[
            jax.ShapeDtypeStruct((plan.halves, 2, 2, plan.block, width), BF16),
            jax.ShapeDtypeStruct((plan.halves, 2, width, plan.block), BF16),
            jax.ShapeDtypeStruct((columns, width), BF16),
        ],
        grid_spec=pltpu.PrefetchScalarGridSpec(
            num_scalar_prefetch=1,
            grid=(plan.halves,),
            in_specs=[
                held,
                held,
                pl.BlockSpec(came.shape, lambda g, w: (0, 0, 0)),
                pl.BlockSpec(teachers.shape, lambda g, w: (0, 0)),
                pl.BlockSpec((width, each), lambda g, w: (0, g)),
            ],
            out_specs=[
                pl.BlockSpec((1, 2, 2, plan.block, width), lambda g, w: (g, 0, 0, 0, 0)),
                pl.BlockSpec((1, 2, width, plan.block), lambda g, w: (g, 0, 0, 0)),
                pl.BlockSpec((each, width), lambda g, w: (g, 0)),
            ],
        ),
        compiler_params=params(50),
        cost_estimate=pl.CostEstimate(
            flops=4 * plan.halves * plan.block * width * teachers.shape[0],
            bytes_accessed=16 * plan.halves * plan.block * width,
            transcendentals=0,
        ),
        name="pair",
    )(where, own, other, came, teachers, weights)


def fill_scale(plan, where, apart, side, first_ref, second_ref, row_factor, scale):
    teachers = plan.tea_lanes * LANES
    places = lax.broadcasted_iota(jnp.int32, (teachers, LANES), 0).astype(F32)
    own_first = jnp.where(where[2] == 0, 0.0, float(teachers // 2))
    for place in range(plan.chips):
        rows = slice(place * plan.stu_count, (place + 1) * plan.stu_count)
        sender = plan.sender(where, apart, side, place)
        total = second_ref[sender, plan.tea_lanes :, :]
        for proto in range(1, plan.protos):
            total = total + second_ref[sender + proto, plan.tea_lanes :, :]
        scale[0, rows, :] = as_columns((loss_scale / student_temp) / total)
        index = first_ref[sender, plan.tea_lanes :, :] + own_first
        index = jnp.where(index >= teachers, index - teachers, index)
        found = [
            jnp.sum(jnp.where(index[i : i + 1] == places, row_factor[...], 0.0), 0, keepdims=True)
            for i in range(plan.stu_lanes)
        ]
        scale[1, rows, :] = as_columns(jnp.concatenate(found, 0))


def gradient_products(
    both_ref, turned_ref, factor_ref, weights_ref, flipped_ref, shares_ref, scale, grads, sub,
    earlier,
):
    columns = weights_ref.shape[1]
    tile = tile_of(columns, 8 * sub)

    def products(step, shares):
        base = pl.multiple_of(step * tile, tile)

        def logits(start):
            weights = weights_ref[:, pl.ds(base + start, sub)]
            return dot(both_ref[0, 0, 0], weights), dot(both_ref[0, 0, 1], weights)

        ahead = logits(0)
        for start in range(0, tile, sub):
            student, target = ahead
            if start + sub < tile:
                ahead = logits(start + sub)
            span = pl.ds(base + start, sub)
            student = jnp.exp2(student * (LOG2E / student_temp)) * widen(scale[0], sub)
            target = jnp.exp2(target * (LOG2E / teacher_temp)) * (
                widen(scale[1], sub) * factor_ref[:, span]
            )
            grad = (student - target).astype(BF16)
            if shares_ref is not None:
                share = dot(grad, flipped_ref[span, :])
                shares = share if shares is None else shares + share
            share = dot(turned_ref[0, 0], grad)
            grads[:, span] = earlier(span) + share
        return shares

    @pl.loop(0, columns // tile)
    def _(step):
        shares = products(step, None)
        if shares_ref is not None:
            shares_ref[...] += shares


def near_kernel(
    where_ref,
    both_ref,
    turned_ref,
    first_ref,
    second_ref,
    factor_ref,
    weights_ref,
    flipped_ref,
    own_raw_ref,
    other_raw_ref,
    own_ref,
    other_ref,
    grads_ref,
    scale,
    shares,
    row_factor,
    *,
    plan,
    sub,
):
    where = (where_ref[0], where_ref[1], where_ref[2])
    part, side = pl.program_id(0), pl.program_id(1)
    count = plan.stu_count

    @pl.when((part == 0) & (side == 0))
    def _():
        row_factor[...] = as_columns(
            (loss_scale / student_temp) / plan.teacher_totals(where, second_ref)
        )

    @pl.when(part == 0)
    def _():
        fill_scale(plan, where, 0, side, first_ref, second_ref, row_factor, scale.at[side])
        shares[side] = jnp.zeros(shares.shape[1:], F32)

    gradient_products(
        both_ref, turned_ref, factor_ref, weights_ref, flipped_ref, shares.at[side],
        scale.at[side], grads_ref, sub, lambda span: jnp.where(side == 0, 0.0, grads_ref[:, span]),
    )

    def finish(raw_ref, out_ref):
        for place in range(plan.chips):
            rows = slice(place * count, (place + 1) * count)
            chip = where[1] ^ reverse_bits(place, plan.chips)
            unit = unit_rows(raw_ref[place, 0])
            share = shares[side, rows, :]
            share = share - unit * jnp.sum(unit * share, 1, keepdims=True)
            out_ref[pl.ds(pl.multiple_of(chip * count, count), count), :] = share

    @pl.when((part == pl.num_programs(0) - 1) & (side == 0))
    def _():
        finish(own_raw_ref, own_ref)

    @pl.when((part == pl.num_programs(0) - 1) & (side == 1))
    def _():
        finish(other_raw_ref, other_ref)


def whole_spec(array):
    return pl.BlockSpec(
        array.shape, lambda q, p, w: (0,) * array.ndim, pipeline_mode=pl.Buffered(1)
    )


def parts_of(columns):
    return 2 if columns % (2 * LANES) == 0 else 1


def near_gradients(plan, where, both, turned, first, second, factor, weights, flipped, own, other):
    width, columns = weights.shape
    parts = parts_of(columns)
    each = columns // parts
    last = plan.halves - 1
    rows = pl.BlockSpec((1, 1, 2, plan.block, width), lambda q, p, w: (last, p, 0, 0, 0))
    across = pl.BlockSpec((width, each), lambda q, p, w: (0, q))
    raw = pl.BlockSpec(
        (plan.chips, 1, plan.stu_count, width),
        lambda q, p, w: (0, 0, 0, 0),
        pipeline_mode=pl.Buffered(1),
    )
    students = jax.ShapeDtypeStruct((plan.block, width), F32)
    return pl.pallas_call(
        functools.partial(near_kernel, plan=plan, sub=tile_of(each, 256)),
        out_shape=[students, students, jax.ShapeDtypeStruct((width, columns), F32)],
        grid_spec=pltpu.PrefetchScalarGridSpec(
            num_scalar_prefetch=1,
            grid=(parts, 2),
            in_specs=[
                rows,
                pl.BlockSpec((1, 1, width, plan.block), lambda q, p, w: (last, p, 0, 0)),
                whole_spec(first),
                whole_spec(second),
                pl.BlockSpec((1, each), lambda q, p, w: (0, q)),
                across,
                pl.BlockSpec((each, width), lambda q, p, w: (q, 0)),
                raw,
                raw,
            ],
            out_specs=[whole_spec(students), whole_spec(students), across],
            scratch_shapes=[
                pltpu.VMEM((2, 2, plan.block, LANES), F32),
                pltpu.VMEM((2, plan.block, width), F32),
                pltpu.VMEM((plan.tea_lanes * LANES, LANES), F32),
            ],
        ),
        compiler_params=params(50, 2),
        cost_estimate=pl.CostEstimate(
            flops=16 * plan.block * width * columns,
            bytes_accessed=8 * width * columns,
            transcendentals=4 * plan.block * columns,
        ),
        name="near_gradients",
    )(where, both, turned, first, second, factor, weights, flipped, own, other)


def far_kernel(
    where_ref,
    both_ref,
    turned_ref,
    first_ref,
    second_ref,
    factor_ref,
    weights_ref,
    raw_ref,
    norm_ref,
    before_ref,
    proto_ref,
    scale,
    grads,
    row_factor,
    *,
    plan,
    sub,
):
    where = (where_ref[0], where_ref[1], where_ref[2])
    part, block = pl.program_id(0), pl.program_id(1)
    columns = weights_ref.shape[1]

    @pl.when((part == 0) & (block == 0))
    def _():
        row_factor[...] = as_columns(
            (loss_scale / student_temp) / plan.teacher_totals(where, second_ref)
        )

    @pl.when(part == 0)
    def _():
        apart = plan.halves - 1 - block // 2
        fill_scale(
            plan, where, apart, block % 2, first_ref, second_ref, row_factor, scale.at[block]
        )

    gradient_products(
        both_ref, turned_ref, factor_ref, weights_ref, None, None, scale.at[block],
        grads, sub, lambda span: jnp.where(block == 0, before_ref[:, span], grads[:, span]),
    )

    @pl.when(block == pl.num_programs(1) - 1)
    def _():
        kept = grads.shape[0] // plan.halves
        mine = pl.ds(pl.multiple_of(where[0] * kept, kept), kept)
        largest = jnp.zeros((kept, LANES), F32)
        for start in range(0, columns, sub):
            span = slice(start, start + sub)
            inverse = 1.0 / norm_ref[:, span]
            unit = raw_ref[:, span].astype(F32) * inverse
            along = jnp.sum(unit * grads[:, span], 0, keepdims=True)
            unit = raw_ref[mine, span].astype(F32) * inverse
            ready = (grads[mine, span] - unit * along) * inverse
            proto_ref[:, span] = ready
            ready = jnp.abs(ready)
            for i in range(0, sub, LANES):
                largest = jnp.maximum(largest, ready[:, i : i + LANES])
        largest = jnp.maximum(jnp.max(jnp.max(largest, 0, keepdims=True), 1, keepdims=True), 1e-30)
        power = jnp.floor(jnp.log2(largest)) - 13.0
        shrink = jnp.exp2(-power)
        for start in range(0, columns, sub):
            span = slice(start, start + sub)
            proto_ref[:, span] = proto_ref[:, span] * shrink
        proto_ref[:, columns:] = jnp.broadcast_to(power, (kept, LANES))


def far_gradients(
    plan, where, both, turned, first, second, factor, weights, prototypes, norm, before
):
    width, columns = weights.shape
    parts = parts_of(columns)
    each = columns // parts
    blocks = 2 * (plan.halves - 1)
    kept = width // plan.halves
    rows = pl.BlockSpec((1, 1, 2, plan.block, width), lambda q, p, w: (p // 2, p % 2, 0, 0, 0))
    across = pl.BlockSpec((width, each), lambda q, p, w: (0, q))
    thin = pl.BlockSpec((1, each), lambda q, p, w: (0, q))
    return pl.pallas_call(
        functools.partial(far_kernel, plan=plan, sub=tile_of(each, 256)),
        out_shape=jax.ShapeDtypeStruct((kept, parts * (each + LANES)), F32),
        grid_spec=pltpu.PrefetchScalarGridSpec(
            num_scalar_prefetch=1,
            grid=(parts, blocks),
            in_specs=[
                rows,
                pl.BlockSpec((1, 1, width, plan.block), lambda q, p, w: (p // 2, p % 2, 0, 0)),
                whole_spec(first),
                whole_spec(second),
                thin,
                across,
                pl.BlockSpec((width, each), lambda q, p, w: (0, (w[1] * 2 + w[2]) * parts + q)),
                thin,
                across,
            ],
            out_specs=pl.BlockSpec((kept, each + LANES), lambda q, p, w: (0, q)),
            scratch_shapes=[
                pltpu.VMEM((blocks, 2, plan.block, LANES), F32),
                pltpu.VMEM((width, each), F32),
                pltpu.VMEM((plan.tea_lanes * LANES, LANES), F32),
            ],
        ),
        compiler_params=params(46, 2),
        cost_estimate=pl.CostEstimate(
            flops=12 * (plan.halves - 1) * plan.block * width * columns,
            bytes_accessed=8 * width * columns,
            transcendentals=4 * (plan.halves - 1) * plan.block * columns,
        ),
        name="far_gradients",
    )(where, both, turned, first, second, factor, weights, prototypes, norm, before)


def join_kernel(came_ref, out_ref, *, parts):
    count, _, length = came_ref.shape
    step = length // parts
    columns = step - LANES
    for number in range(count * parts):
        sender, start = number // parts, number % parts * step
        factor = jnp.exp2(came_ref[sender, :, start + columns : start + step])
        out_ref[:, number * columns : (number + 1) * columns] = came_ref[
            sender, :, start : start + columns
        ] * widen(factor, columns)


def join(came, parts):
    senders, share, length = came.shape
    columns = length - parts * LANES
    each = tile_of(senders, 2)
    return pl.pallas_call(
        functools.partial(join_kernel, parts=parts),
        out_shape=jax.ShapeDtypeStruct((share, senders * columns), F32),
        grid=(senders // each,),
        in_specs=[pl.BlockSpec((each, share, length), lambda i: (i, 0, 0))],
        out_specs=pl.BlockSpec((share, each * columns), lambda i: (0, i)),
        compiler_params=params(16),
        cost_estimate=pl.CostEstimate(
            flops=share * senders * columns,
            bytes_accessed=8 * share * senders * columns,
            transcendentals=0,
        ),
        name="join",
    )(came)


def swap(value, axis):
    return lax.ppermute(value, axis, [(0, 1), (1, 0)])


def exchange(value, axes):
    return lax.all_to_all(value, axes, split_axis=0, concat_axis=0, tiled=True)


def gather(value, axes, count):
    return exchange(jnp.tile(value, (count,) + (1,) * (value.ndim - 1)), axes)


def tie(value, *others):
    return lax.optimization_barrier((value,) + others)[0]


def body(teacher, students, prototypes, pairing, layout):
    halves, chips, protos = lax.axis_size("half"), lax.axis_size("chip"), lax.axis_size("protos")
    half, chip, core, proto = (lax.axis_index(a) for a in ("half", "chip", "core", "protos"))
    everyone = ("half", "chip", "core", "protos")
    all_chips = halves * chips
    width, held = prototypes.shape
    tea_count, stu_count = teacher.shape[0], students.shape[0]
    plan = Layout(halves, chips, protos, tea_count, stu_count)
    columns = held // (chips * 2)
    part_columns = columns // halves
    where = jnp.stack([half, chip, core]).astype(jnp.int32)
    parcel = lambda lanes: jax.ShapeDtypeStruct((plan.devices, lanes, LANES), F32)

    tiled = jnp.tile(teacher, (all_chips, 1))
    tea_own = exchange(tiled, ("half", "chip"))
    weights, norm, near_total = local_denominator(
        tie(where, tiled), students, prototypes, 0, 1, 4, columns
    )
    tea_other = swap(tea_own, "core")
    parcel_one, tea_unit, mark = sweep_call(
        first_sweep_kernel,
        plan,
        tie(where, near_total),
        [tea_own, tea_other, weights, pairing.reshape(1, -1), layout.reshape(1, -1)],
        2,
        part_columns,
        [
            parcel(plan.tea_lanes + plan.stu_lanes),
            jax.ShapeDtypeStruct((2 * plan.tea_rows, width), BF16),
            jax.ShapeDtypeStruct((8, LANES), F32),
        ],
        "first_sweep",
    )
    first = exchange(parcel_one, everyone)
    (far_total,) = local_denominator(tie(where, mark), students, prototypes, 1, 3, 4)

    markers = [near_total, mark, far_total]
    gathered = tie(students, tiled)[None]
    bit = all_chips // 2
    while bit:
        came = lax.ppermute(
            gathered, ("half", "chip"), [(q, q ^ bit) for q in range(all_chips)]
        )
        if markers:
            came = tie(came, markers.pop(0))
        gathered = jnp.concatenate([gathered, came], 0)
        bit //= 2
    stu_own = gathered.reshape(chips, halves, stu_count, width)
    stu_other = swap(stu_own, "core")

    parcel_two, factor = sweep_call(
        second_sweep_kernel,
        plan,
        where,
        [tea_unit, weights, first, near_total, far_total],
        1,
        part_columns,
        [
            parcel(plan.tea_lanes + plan.stu_lanes),
            jax.ShapeDtypeStruct((1, part_columns), F32),
        ],
        "second_sweep",
    )
    second = exchange(parcel_two, everyone)
    both, turned, flipped = pair(
        plan, where, stu_own, stu_other, tie(first, parcel_two), tea_unit, weights
    )
    second, both, turned, flipped = lax.optimization_barrier((second, both, turned, flipped))
    factors = [factor]
    for step in range(1, halves):
        factors.append(
            lax.ppermute(factor, "half", [(h, (h + step) % halves) for h in range(halves)])
        )
    if halves == 2:
        factors = [jnp.where(half == step, factors[0], factors[1]) for step in range(2)]
    elif halves > 2:
        factors = [jnp.stack(factors)[(half - step) % halves] for step in range(halves)]
    factor = jnp.concatenate(factors, 1)

    rows_of = (both, turned, first, second, factor, weights)
    own_part, other_part, proto_all = near_gradients(
        plan, where, *rows_of, flipped, stu_own, stu_other
    )
    split = (chips, 1, protos, stu_count // protos, width)
    sides = [
        jnp.where(core == side, own_part, other_part).reshape(split) for side in range(2)
    ]
    sent = (jnp.concatenate(sides, 1) * 128.0).astype(F16)
    sent = sent.reshape(chips * 2 * protos, stu_count // protos, width)
    came = exchange(sent, ("chip", "core", "protos"))
    proto_part = far_gradients(plan, tie(where, sent), *rows_of, prototypes, norm, proto_all)
    share = width // (all_chips * 2)
    sent = proto_part.astype(F16).reshape(chips * 2, share, -1)
    grad_protos = join(exchange(sent, ("chip", "core")).astype(F32), parts_of(columns))

    rows = jnp.sum(came.astype(F32), 0) * (1.0 / 128.0)
    if protos == 2:
        far = swap(rows, "protos")
        grad_unit = jnp.concatenate(
            [jnp.where(proto == 0, rows, far), jnp.where(proto == 0, far, rows)], 0
        )
    else:
        grad_unit = gather(rows, "protos", protos)
    stu_full = students.astype(F32)
    u_norm = jnp.sqrt(jnp.sum(stu_full * stu_full, 1, keepdims=True) + epsilon)
    return (grad_unit / u_norm, grad_protos)


def solution(mesh):
    rows, protos = mesh.shape["rows"], mesh.shape["protos"]
    halves = HALVES
    split = Mesh(
        mesh.devices.reshape(halves, rows // (2 * halves), 2, protos),
        ("half", "chip", "core", "protos"),
    )
    over_rows = ("half", "chip", "core")
    in_specs = (
        P(over_rows, None),
        P(over_rows, None),
        P(None, "protos"),
        P(over_rows),
        P(over_rows),
    )
    out_specs = (P(over_rows, None), P(over_rows, "protos"))
    return jax.shard_map(
        body, mesh=split, in_specs=in_specs, out_specs=out_specs, check_vma=False
    )
```

```python
import functools

import jax
import jax.numpy as jnp
from jax import lax
from jax.experimental import pallas as pl
from jax.experimental.pallas import tpu as pltpu
from jax.sharding import Mesh, PartitionSpec as P

epsilon = 1e-06
teacher_temp = 0.07
student_temp = 0.1
loss_scale = 16.0

LOG2E = 1.4426950408889634
HALVES = 2
LANES = 128
MIB = 1024 * 1024
F32 = jnp.float32
BF16 = jnp.bfloat16
F16 = jnp.float16


def params(limit, grid=1):
    return pltpu.CompilerParams(
        vmem_limit_bytes=limit * MIB, dimension_semantics=("arbitrary",) * grid
    )


def tile_of(size, want):
    return want if size % want == 0 else size


def unit_rows(rows):
    full = rows.astype(F32)
    return full * (1.0 / jnp.sqrt(jnp.sum(full * full, 1, keepdims=True) + epsilon))


def lane_fold(block):
    total = block[:, :LANES]
    for start in range(LANES, block.shape[1], LANES):
        total = total + block[:, start : start + LANES]
    return total


def widen(column, width):
    return jnp.concatenate([column] * (width // LANES), 1)


def as_columns(values):
    return jnp.concatenate(
        [
            jnp.transpose(jnp.broadcast_to(values[i : i + 1], (LANES, LANES)))
            for i in range(values.shape[0])
        ],
        0,
    )


def as_rows(folded):
    return jnp.concatenate(
        [
            jnp.sum(jnp.transpose(folded[i : i + LANES]), 0, keepdims=True)
            for i in range(0, folded.shape[0], LANES)
        ],
        0,
    )


def dot(a, b):
    return jnp.dot(a, b, preferred_element_type=F32)


def reverse_bits(place, count):
    bits = count.bit_length() - 1
    return sum(((place >> i) & 1) << (bits - 1 - i) for i in range(bits))


class Layout:
    def __init__(self, halves, chips, protos, tea_count, stu_count):
        self.halves, self.chips, self.protos = halves, chips, protos
        self.devices = halves * chips * 2 * protos
        self.tea_rows = halves * chips * tea_count
        self.tea_lanes = 2 * self.tea_rows // LANES
        self.stu_lanes = stu_count // LANES
        self.stu_count = stu_count
        self.block = chips * stu_count

    def sender(self, where, other_half, other_core, place):
        half, chip, core = where[0], where[1], where[2]
        source = (half ^ other_half) * self.chips + (chip ^ reverse_bits(place, self.chips))
        return (source * 2 + (core ^ other_core)) * self.protos

    def teacher_totals(self, where, parcels_ref):
        sums = [None, None]
        for number in range(self.devices):
            side = (number // self.protos) % 2
            piece = parcels_ref[number, : self.tea_lanes]
            sums[side] = piece if sums[side] is None else sums[side] + piece
        cut = self.tea_lanes // 2
        turned = [jnp.concatenate([s[cut:], s[:cut]], 0) for s in sums]
        return jnp.where(where[2] == 0, sums[0] + turned[1], sums[1] + turned[0])


def denominator_kernel(where_ref, students_ref, weights_ref, *refs, sub):
    total_ref, unit, folded = refs[-3:]
    step = pl.program_id(0)

    if len(refs) > 3:
        raw_ref, unit_ref, norm_ref = refs[:3]
        full = raw_ref[...].astype(F32)
        norm = jnp.sqrt(jnp.sum(full * full, 0, keepdims=True) + epsilon)
        unit_ref[...] = (full * (1.0 / norm)).astype(BF16)
        norm_ref[...] = norm

    @pl.when(step == 0)
    def _():
        unit[...] = unit_rows(students_ref[...]).astype(BF16)
        folded[...] = jnp.zeros_like(folded)

    def scaled(start):
        weights = weights_ref[:, start : start + sub].astype(F32)
        inverse = 1.0 / jnp.sqrt(jnp.sum(weights * weights, 0, keepdims=True) + epsilon)
        return (weights * inverse).astype(BF16)

    total = folded[...]
    for start in range(0, weights_ref.shape[1], sub):
        logits = dot(unit[...], scaled(start))
        total = total + lane_fold(jnp.exp2(logits * (LOG2E / student_temp)))
    folded[...] = total

    @pl.when(step == pl.num_programs(0) - 1)
    def _():
        total_ref[...] = as_rows(folded[...])


def local_denominator(where, students, prototypes, part, count, parts, mine=0):
    rows, width = students.shape
    columns = prototypes.shape[1] // parts
    tile = tile_of(columns, 4096)
    steps = columns // tile
    before = part * steps
    steps, columns = steps * count, columns * count
    in_specs = [
        pl.BlockSpec((rows, width), lambda j, w: (0, 0)),
        pl.BlockSpec((width, tile), lambda j, w: (0, before + j)),
    ]
    out_specs = [pl.BlockSpec((rows // LANES, LANES), lambda j, w: (0, 0))]
    out_shape = [jax.ShapeDtypeStruct((rows // LANES, LANES), F32)]
    operands = [students, prototypes]
    if mine:
        each = mine // steps
        operands.append(prototypes)
        in_specs.append(
            pl.BlockSpec((width, each), lambda j, w: (0, (w[1] * 2 + w[2]) * steps + j))
        )
        out_specs = [
            pl.BlockSpec((width, each), lambda j, w: (0, j)),
            pl.BlockSpec((1, each), lambda j, w: (0, j)),
        ] + out_specs
        out_shape = [
            jax.ShapeDtypeStruct((width, mine), BF16),
            jax.ShapeDtypeStruct((1, mine), F32),
        ] + out_shape
    return pl.pallas_call(
        functools.partial(denominator_kernel, sub=tile_of(tile, 512)),
        out_shape=out_shape,
        grid_spec=pltpu.PrefetchScalarGridSpec(
            num_scalar_prefetch=1,
            grid=(steps,),
            in_specs=in_specs,
            out_specs=out_specs,
            scratch_shapes=[pltpu.VMEM((rows, width), BF16), pltpu.VMEM((rows, LANES), F32)],
        ),
        compiler_params=params(50),
        cost_estimate=pl.CostEstimate(
            flops=2 * rows * width * columns,
            bytes_accessed=2 * width * columns,
            transcendentals=rows * columns,
        ),
        name="denominator",
    )(where, *operands)


def sweep_totals(units, weights_ref, column, sub, factor_ref):
    folded = jnp.zeros((units.shape[0], LANES), F32)
    for start in range(0, weights_ref.shape[1], sub):
        scores = jnp.exp2(dot(units, weights_ref[:, start : start + sub]) * (LOG2E / teacher_temp))
        weighted = scores if column is None else scores * widen(column, sub)
        factor = 1.0 / jnp.sum(weighted, 0, keepdims=True)
        if factor_ref is not None:
            factor_ref[:, start : start + sub] = factor
        folded = folded + lane_fold(scores * factor)
    return as_rows(folded)


def first_sweep_kernel(
    where_ref, own_ref, other_ref, weights_ref, pairing_ref, layout_ref, parcel_ref, unit_ref, mark_ref, *, plan, sub
):
    mark_ref[...] = jnp.zeros_like(mark_ref)
    half = own_ref.shape[0]
    unit_ref[:half, :] = unit_rows(own_ref[...]).astype(BF16)
    unit_ref[half:, :] = unit_rows(other_ref[...]).astype(BF16)
    totals = sweep_totals(unit_ref[...], weights_ref, None, sub, None)
    parcel_ref[:, : plan.tea_lanes, :] = jnp.broadcast_to(
        totals[None], (plan.devices,) + totals.shape
    )
    each = plan.tea_rows // (plan.halves * plan.chips)
    layout = layout_ref[...]
    index = (layout & 1) * half + (layout >> 1) * each + pairing_ref[...]
    index = index.astype(F32)
    for i in range(plan.stu_lanes):
        parcel_ref[:, plan.tea_lanes + i, :] = jnp.broadcast_to(
            index[:, i * LANES : (i + 1) * LANES], (plan.devices, LANES)
        )


def second_sweep_kernel(
    where_ref, unit_ref, weights_ref, came_ref, near_ref, far_ref, parcel_ref, factor_ref, *, plan, sub
):
    where = (where_ref[0], where_ref[1], where_ref[2])
    column = as_columns(1.0 / plan.teacher_totals(where, came_ref))
    totals = sweep_totals(unit_ref[...], weights_ref, column, sub, factor_ref)
    totals = jnp.concatenate([totals, near_ref[...] + far_ref[...]], 0)
    parcel_ref[...] = jnp.broadcast_to(totals[None], (plan.devices,) + totals.shape)


def sweep_call(kernel, plan, where, operands, weights_at, columns, out_shape, name):
    width = operands[0].shape[1]

    def spec(number, array):
        if number == weights_at:
            return pl.BlockSpec((width, columns), lambda i, w: (0, w[0]))
        return pl.BlockSpec(array.shape, lambda i, w: (0,) * len(array.shape))

    return pl.pallas_call(
        functools.partial(kernel, plan=plan, sub=tile_of(columns, 256)),
        out_shape=out_shape,
        grid_spec=pltpu.PrefetchScalarGridSpec(
            num_scalar_prefetch=1,
            grid=(1,),
            in_specs=[spec(i, a) for i, a in enumerate(operands)],
            out_specs=[
                pl.BlockSpec(o.shape, functools.partial(lambda n, i, w: (0,) * n, len(o.shape)))
                for o in out_shape
            ],
        ),
        compiler_params=params(16),
        cost_estimate=pl.CostEstimate(
            flops=4 * plan.tea_rows * width * columns,
            bytes_accessed=2 * width * (columns + 2 * plan.tea_rows),
            transcendentals=2 * plan.tea_rows * columns,
        ),
        name=name,
    )(where, *operands)


def pair_kernel(
    where_ref, own_ref, other_ref, came_ref, teacher_ref, weights_ref, both_ref, turned_ref,
    flipped_ref, *, plan
):
    where = (where_ref[0], where_ref[1], where_ref[2])
    apart = plan.halves - 1 - pl.program_id(0)
    teachers = teacher_ref.shape[0]
    count = plan.stu_count
    lane = lax.broadcasted_iota(jnp.int32, (count, LANES), 1).astype(F32)
    flipped_ref[...] = jnp.transpose(weights_ref[...])
    for side, ref in enumerate((own_ref, other_ref)):
        for place in range(plan.chips):
            rows = slice(place * count, (place + 1) * count)
            unit = unit_rows(ref[place, 0]).astype(BF16)
            both_ref[0, side, 0, rows, :] = unit
            turned_ref[0, side, :, rows] = jnp.transpose(unit)
            sender = plan.sender(where, apart, side, place)
            index = as_columns(came_ref[sender, plan.tea_lanes :, :])
            index = index + jnp.where(where[2] == 0, 0.0, float(teachers // 2))
            index = jnp.where(index >= teachers, index - teachers, index)
            chosen = jnp.concatenate(
                [
                    jnp.where(index == lane + start, 1.0, 0.0).astype(BF16)
                    for start in range(0, teachers, LANES)
                ],
                1,
            )
            both_ref[0, side, 1, rows, :] = dot(chosen, teacher_ref[...]).astype(BF16)


def pair(plan, where, own, other, came, teachers, weights):
    width, columns = weights.shape
    each = columns // plan.halves
    held = pl.BlockSpec(
        (plan.chips, 1, plan.stu_count, width), lambda g, w: (0, plan.halves - 1 - g, 0, 0)
    )
    return pl.pallas_call(
        functools.partial(pair_kernel, plan=plan),
        out_shape=[
            jax.ShapeDtypeStruct((plan.halves, 2, 2, plan.block, width), BF16),
            jax.ShapeDtypeStruct((plan.halves, 2, width, plan.block), BF16),
            jax.ShapeDtypeStruct((columns, width), BF16),
        ],
        grid_spec=pltpu.PrefetchScalarGridSpec(
            num_scalar_prefetch=1,
            grid=(plan.halves,),
            in_specs=[
                held,
                held,
                pl.BlockSpec(came.shape, lambda g, w: (0, 0, 0)),
                pl.BlockSpec(teachers.shape, lambda g, w: (0, 0)),
                pl.BlockSpec((width, each), lambda g, w: (0, g)),
            ],
            out_specs=[
                pl.BlockSpec((1, 2, 2, plan.block, width), lambda g, w: (g, 0, 0, 0, 0)),
                pl.BlockSpec((1, 2, width, plan.block), lambda g, w: (g, 0, 0, 0)),
                pl.BlockSpec((each, width), lambda g, w: (g, 0)),
            ],
        ),
        compiler_params=params(50),
        cost_estimate=pl.CostEstimate(
            flops=4 * plan.halves * plan.block * width * teachers.shape[0],
            bytes_accessed=16 * plan.halves * plan.block * width,
            transcendentals=0,
        ),
        name="pair",
    )(where, own, other, came, teachers, weights)


def fill_scale(plan, where, apart, side, first_ref, second_ref, row_factor, scale):
    teachers = plan.tea_lanes * LANES
    places = lax.broadcasted_iota(jnp.int32, (teachers, LANES), 0).astype(F32)
    own_first = jnp.where(where[2] == 0, 0.0, float(teachers // 2))
    for place in range(plan.chips):
        rows = slice(place * plan.stu_count, (place + 1) * plan.stu_count)
        sender = plan.sender(where, apart, side, place)
        total = second_ref[sender, plan.tea_lanes :, :]
        for proto in range(1, plan.protos):
            total = total + second_ref[sender + proto, plan.tea_lanes :, :]
        scale[0, rows, :] = as_columns((loss_scale / student_temp) / total)
        index = first_ref[sender, plan.tea_lanes :, :] + own_first
        index = jnp.where(index >= teachers, index - teachers, index)
        found = [
            jnp.sum(jnp.where(index[i : i + 1] == places, row_factor[...], 0.0), 0, keepdims=True)
            for i in range(plan.stu_lanes)
        ]
        scale[1, rows, :] = as_columns(jnp.concatenate(found, 0))


def gradient_products(
    both_ref, turned_ref, factor_ref, weights_ref, flipped_ref, shares_ref, scale, grads, sub,
    earlier,
):
    columns = weights_ref.shape[1]
    tile = tile_of(columns, 8 * sub)

    def products(step, shares):
        base = pl.multiple_of(step * tile, tile)

        def logits(start):
            weights = weights_ref[:, pl.ds(base + start, sub)]
            return dot(both_ref[0, 0, 0], weights), dot(both_ref[0, 0, 1], weights)

        ahead = logits(0)
        for start in range(0, tile, sub):
            student, target = ahead
            if start + sub < tile:
                ahead = logits(start + sub)
            span = pl.ds(base + start, sub)
            student = jnp.exp2(student * (LOG2E / student_temp)) * widen(scale[0], sub)
            target = jnp.exp2(target * (LOG2E / teacher_temp)) * (
                widen(scale[1], sub) * factor_ref[:, span]
            )
            grad = (student - target).astype(BF16)
            if shares_ref is not None:
                share = dot(grad, flipped_ref[span, :])
                shares = share if shares is None else shares + share
            share = dot(turned_ref[0, 0], grad)
            grads[:, span] = earlier(span) + share
        return shares

    @pl.loop(0, columns // tile)
    def _(step):
        shares = products(step, None)
        if shares_ref is not None:
            shares_ref[...] += shares


def near_kernel(
    where_ref,
    both_ref,
    turned_ref,
    first_ref,
    second_ref,
    factor_ref,
    weights_ref,
    flipped_ref,
    own_raw_ref,
    other_raw_ref,
    own_ref,
    other_ref,
    grads_ref,
    scale,
    shares,
    row_factor,
    *,
    plan,
    sub,
):
    where = (where_ref[0], where_ref[1], where_ref[2])
    part, side = pl.program_id(0), pl.program_id(1)
    count = plan.stu_count

    @pl.when((part == 0) & (side == 0))
    def _():
        row_factor[...] = as_columns(
            (loss_scale / student_temp) / plan.teacher_totals(where, second_ref)
        )

    @pl.when(part == 0)
    def _():
        fill_scale(plan, where, 0, side, first_ref, second_ref, row_factor, scale.at[side])
        shares[side] = jnp.zeros(shares.shape[1:], F32)

    gradient_products(
        both_ref, turned_ref, factor_ref, weights_ref, flipped_ref, shares.at[side],
        scale.at[side], grads_ref, sub, lambda span: jnp.where(side == 0, 0.0, grads_ref[:, span]),
    )

    def finish(raw_ref, out_ref):
        for place in range(plan.chips):
            rows = slice(place * count, (place + 1) * count)
            chip = where[1] ^ reverse_bits(place, plan.chips)
            unit = unit_rows(raw_ref[place, 0])
            share = shares[side, rows, :]
            share = share - unit * jnp.sum(unit * share, 1, keepdims=True)
            out_ref[pl.ds(pl.multiple_of(chip * count, count), count), :] = share

    @pl.when((part == pl.num_programs(0) - 1) & (side == 0))
    def _():
        finish(own_raw_ref, own_ref)

    @pl.when((part == pl.num_programs(0) - 1) & (side == 1))
    def _():
        finish(other_raw_ref, other_ref)


def whole_spec(array):
    return pl.BlockSpec(
        array.shape, lambda q, p, w: (0,) * array.ndim, pipeline_mode=pl.Buffered(1)
    )


def parts_of(columns):
    return 2 if columns % (2 * LANES) == 0 else 1


def near_gradients(plan, where, both, turned, first, second, factor, weights, flipped, own, other):
    width, columns = weights.shape
    parts = parts_of(columns)
    each = columns // parts
    last = plan.halves - 1
    rows = pl.BlockSpec((1, 1, 2, plan.block, width), lambda q, p, w: (last, p, 0, 0, 0))
    across = pl.BlockSpec((width, each), lambda q, p, w: (0, q))
    raw = pl.BlockSpec(
        (plan.chips, 1, plan.stu_count, width),
        lambda q, p, w: (0, 0, 0, 0),
        pipeline_mode=pl.Buffered(1),
    )
    students = jax.ShapeDtypeStruct((plan.block, width), F32)
    return pl.pallas_call(
        functools.partial(near_kernel, plan=plan, sub=tile_of(each, 256)),
        out_shape=[students, students, jax.ShapeDtypeStruct((width, columns), F32)],
        grid_spec=pltpu.PrefetchScalarGridSpec(
            num_scalar_prefetch=1,
            grid=(parts, 2),
            in_specs=[
                rows,
                pl.BlockSpec((1, 1, width, plan.block), lambda q, p, w: (last, p, 0, 0)),
                whole_spec(first),
                whole_spec(second),
                pl.BlockSpec((1, each), lambda q, p, w: (0, q)),
                across,
                pl.BlockSpec((each, width), lambda q, p, w: (q, 0)),
                raw,
                raw,
            ],
            out_specs=[whole_spec(students), whole_spec(students), across],
            scratch_shapes=[
                pltpu.VMEM((2, 2, plan.block, LANES), F32),
                pltpu.VMEM((2, plan.block, width), F32),
                pltpu.VMEM((plan.tea_lanes * LANES, LANES), F32),
            ],
        ),
        compiler_params=params(50, 2),
        cost_estimate=pl.CostEstimate(
            flops=16 * plan.block * width * columns,
            bytes_accessed=8 * width * columns,
            transcendentals=4 * plan.block * columns,
        ),
        name="near_gradients",
    )(where, both, turned, first, second, factor, weights, flipped, own, other)


def far_kernel(
    where_ref,
    both_ref,
    turned_ref,
    first_ref,
    second_ref,
    factor_ref,
    weights_ref,
    raw_ref,
    norm_ref,
    before_ref,
    proto_ref,
    scale,
    grads,
    row_factor,
    *,
    plan,
    sub,
):
    where = (where_ref[0], where_ref[1], where_ref[2])
    part, block = pl.program_id(0), pl.program_id(1)
    columns = weights_ref.shape[1]

    @pl.when((part == 0) & (block == 0))
    def _():
        row_factor[...] = as_columns(
            (loss_scale / student_temp) / plan.teacher_totals(where, second_ref)
        )

    @pl.when(part == 0)
    def _():
        apart = plan.halves - 1 - block // 2
        fill_scale(
            plan, where, apart, block % 2, first_ref, second_ref, row_factor, scale.at[block]
        )

    gradient_products(
        both_ref, turned_ref, factor_ref, weights_ref, None, None, scale.at[block],
        grads, sub, lambda span: jnp.where(block == 0, before_ref[:, span], grads[:, span]),
    )

    @pl.when(block == pl.num_programs(1) - 1)
    def _():
        kept = grads.shape[0] // plan.halves
        mine = pl.ds(pl.multiple_of(where[0] * kept, kept), kept)
        largest = jnp.zeros((kept, LANES), F32)
        for start in range(0, columns, sub):
            span = slice(start, start + sub)
            inverse = 1.0 / norm_ref[:, span]
            unit = raw_ref[:, span].astype(F32) * inverse
            along = jnp.sum(unit * grads[:, span], 0, keepdims=True)
            unit = raw_ref[mine, span].astype(F32) * inverse
            ready = (grads[mine, span] - unit * along) * inverse
            proto_ref[:, span] = ready
            ready = jnp.abs(ready)
            for i in range(0, sub, LANES):
                largest = jnp.maximum(largest, ready[:, i : i + LANES])
        largest = jnp.maximum(jnp.max(jnp.max(largest, 0, keepdims=True), 1, keepdims=True), 1e-30)
        power = jnp.floor(jnp.log2(largest)) - 13.0
        shrink = jnp.exp2(-power)
        for start in range(0, columns, sub):
            span = slice(start, start + sub)
            proto_ref[:, span] = proto_ref[:, span] * shrink
        proto_ref[:, columns:] = jnp.broadcast_to(power, (kept, LANES))


def far_gradients(
    plan, where, both, turned, first, second, factor, weights, prototypes, norm, before
):
    width, columns = weights.shape
    parts = parts_of(columns)
    each = columns // parts
    blocks = 2 * (plan.halves - 1)
    kept = width // plan.halves
    rows = pl.BlockSpec((1, 1, 2, plan.block, width), lambda q, p, w: (p // 2, p % 2, 0, 0, 0))
    across = pl.BlockSpec((width, each), lambda q, p, w: (0, q))
    thin = pl.BlockSpec((1, each), lambda q, p, w: (0, q))
    return pl.pallas_call(
        functools.partial(far_kernel, plan=plan, sub=tile_of(each, 256)),
        out_shape=jax.ShapeDtypeStruct((kept, parts * (each + LANES)), F32),
        grid_spec=pltpu.PrefetchScalarGridSpec(
            num_scalar_prefetch=1,
            grid=(parts, blocks),
            in_specs=[
                rows,
                pl.BlockSpec((1, 1, width, plan.block), lambda q, p, w: (p // 2, p % 2, 0, 0)),
                whole_spec(first),
                whole_spec(second),
                thin,
                across,
                pl.BlockSpec((width, each), lambda q, p, w: (0, (w[1] * 2 + w[2]) * parts + q)),
                thin,
                across,
            ],
            out_specs=pl.BlockSpec((kept, each + LANES), lambda q, p, w: (0, q)),
            scratch_shapes=[
                pltpu.VMEM((blocks, 2, plan.block, LANES), F32),
                pltpu.VMEM((width, each), F32),
                pltpu.VMEM((plan.tea_lanes * LANES, LANES), F32),
            ],
        ),
        compiler_params=params(46, 2),
        cost_estimate=pl.CostEstimate(
            flops=12 * (plan.halves - 1) * plan.block * width * columns,
            bytes_accessed=8 * width * columns,
            transcendentals=4 * (plan.halves - 1) * plan.block * columns,
        ),
        name="far_gradients",
    )(where, both, turned, first, second, factor, weights, prototypes, norm, before)


def join_kernel(came_ref, out_ref, *, parts):
    count, _, length = came_ref.shape
    step = length // parts
    columns = step - LANES
    for number in range(count * parts):
        sender, start = number // parts, number % parts * step
        factor = jnp.exp2(came_ref[sender, :, start + columns : start + step])
        out_ref[:, number * columns : (number + 1) * columns] = came_ref[
            sender, :, start : start + columns
        ] * widen(factor, columns)


def join(came, parts):
    senders, share, length = came.shape
    columns = length - parts * LANES
    each = tile_of(senders, 2)
    return pl.pallas_call(
        functools.partial(join_kernel, parts=parts),
        out_shape=jax.ShapeDtypeStruct((share, senders * columns), F32),
        grid=(senders // each,),
        in_specs=[pl.BlockSpec((each, share, length), lambda i: (i, 0, 0))],
        out_specs=pl.BlockSpec((share, each * columns), lambda i: (0, i)),
        compiler_params=params(16),
        cost_estimate=pl.CostEstimate(
            flops=share * senders * columns,
            bytes_accessed=8 * share * senders * columns,
            transcendentals=0,
        ),
        name="join",
    )(came)


def swap(value, axis):
    return lax.ppermute(value, axis, [(0, 1), (1, 0)])


def exchange(value, axes):
    return lax.all_to_all(value, axes, split_axis=0, concat_axis=0, tiled=True)


def gather(value, axes, count):
    return exchange(jnp.tile(value, (count,) + (1,) * (value.ndim - 1)), axes)


def tie(value, *others):
    return lax.optimization_barrier((value,) + others)[0]


def body(teacher, students, prototypes, pairing, layout):
    halves, chips, protos = lax.axis_size("half"), lax.axis_size("chip"), lax.axis_size("protos")
    half, chip, core, proto = (lax.axis_index(a) for a in ("half", "chip", "core", "protos"))
    everyone = ("half", "chip", "core", "protos")
    all_chips = halves * chips
    width, held = prototypes.shape
    tea_count, stu_count = teacher.shape[0], students.shape[0]
    plan = Layout(halves, chips, protos, tea_count, stu_count)
    columns = held // (chips * 2)
    part_columns = columns // halves
    where = jnp.stack([half, chip, core]).astype(jnp.int32)
    parcel = lambda lanes: jax.ShapeDtypeStruct((plan.devices, lanes, LANES), F32)

    tiled = jnp.tile(teacher, (all_chips, 1))
    tea_own = exchange(tiled, ("half", "chip"))
    weights, norm, near_total = local_denominator(
        where, students, prototypes, 0, 1, 4, columns
    )
    tea_other = swap(tea_own, "core")
    parcel_one, tea_unit, mark = sweep_call(
        first_sweep_kernel,
        plan,
        tie(where, near_total),
        [tea_own, tea_other, weights, pairing.reshape(1, -1), layout.reshape(1, -1)],
        2,
        part_columns,
        [
            parcel(plan.tea_lanes + plan.stu_lanes),
            jax.ShapeDtypeStruct((2 * plan.tea_rows, width), BF16),
            jax.ShapeDtypeStruct((8, LANES), F32),
        ],
        "first_sweep",
    )
    first = exchange(parcel_one, everyone)
    (far_total,) = local_denominator(tie(where, mark), students, prototypes, 1, 3, 4)

    markers = [near_total, mark, far_total]
    gathered = students[None]
    bit = all_chips // 2
    while bit:
        came = lax.ppermute(
            gathered, ("half", "chip"), [(q, q ^ bit) for q in range(all_chips)]
        )
        if markers:
            came = tie(came, markers.pop(0))
        gathered = jnp.concatenate([gathered, came], 0)
        bit //= 2
    stu_own = gathered.reshape(chips, halves, stu_count, width)
    stu_other = swap(stu_own, "core")

    parcel_two, factor = sweep_call(
        second_sweep_kernel,
        plan,
        where,
        [tea_unit, weights, first, near_total, far_total],
        1,
        part_columns,
        [
            parcel(plan.tea_lanes + plan.stu_lanes),
            jax.ShapeDtypeStruct((1, part_columns), F32),
        ],
        "second_sweep",
    )
    second = exchange(parcel_two, everyone)
    both, turned, flipped = pair(
        plan, where, stu_own, stu_other, tie(first, parcel_two), tea_unit, weights
    )
    second, both, turned, flipped = lax.optimization_barrier((second, both, turned, flipped))
    factors = [factor]
    for step in range(1, halves):
        factors.append(
            lax.ppermute(factor, "half", [(h, (h + step) % halves) for h in range(halves)])
        )
    if halves == 2:
        factors = [jnp.where(half == step, factors[0], factors[1]) for step in range(2)]
    elif halves > 2:
        factors = [jnp.stack(factors)[(half - step) % halves] for step in range(halves)]
    factor = jnp.concatenate(factors, 1)

    rows_of = (both, turned, first, second, factor, weights)
    own_part, other_part, proto_all = near_gradients(
        plan, where, *rows_of, flipped, stu_own, stu_other
    )
    split = (chips, 1, protos, stu_count // protos, width)
    sides = [
        jnp.where(core == side, own_part, other_part).reshape(split) for side in range(2)
    ]
    sent = (jnp.concatenate(sides, 1) * 128.0).astype(F16)
    sent = sent.reshape(chips * 2 * protos, stu_count // protos, width)
    came = exchange(sent, ("chip", "core", "protos"))
    proto_part = far_gradients(plan, tie(where, sent), *rows_of, prototypes, norm, proto_all)
    share = width // (all_chips * 2)
    sent = proto_part.astype(F16).reshape(chips * 2, share, -1)
    grad_protos = join(exchange(sent, ("chip", "core")).astype(F32), parts_of(columns))

    rows = jnp.sum(came.astype(F32), 0) * (1.0 / 128.0)
    if protos == 2:
        far = swap(rows, "protos")
        grad_unit = jnp.concatenate(
            [jnp.where(proto == 0, rows, far), jnp.where(proto == 0, far, rows)], 0
        )
    else:
        grad_unit = gather(rows, "protos", protos)
    stu_full = students.astype(F32)
    u_norm = jnp.sqrt(jnp.sum(stu_full * stu_full, 1, keepdims=True) + epsilon)
    return (grad_unit / u_norm, grad_protos)


def solution(mesh):
    rows, protos = mesh.shape["rows"], mesh.shape["protos"]
    halves = HALVES
    split = Mesh(
        mesh.devices.reshape(halves, rows // (2 * halves), 2, protos),
        ("half", "chip", "core", "protos"),
    )
    over_rows = ("half", "chip", "core")
    in_specs = (
        P(over_rows, None),
        P(over_rows, None),
        P(None, "protos"),
        P(over_rows),
        P(over_rows),
    )
    out_specs = (P(over_rows, None), P(over_rows, "protos"))
    return jax.shard_map(
        body, mesh=split, in_specs=in_specs, out_specs=out_specs, check_vma=False
    )
```
